128 devices in a mesh: band: 16 (over x_lo, y, core), dom: 8 (over z, x_hi).
Axes of the slice: x: 4 (x_hi: 2, x_lo: 2; x = x_hi * 2 + x_lo), y: 4, z: 4, core: 2. Of those that a mesh axis runs over, the one named last changes fastest.
Arguments:
- orbitals: bfloat16 [384, 48, 6144], P('band', 'dom'), may hold values from -6 to 6
- potential: float32 [48, 6144], P('dom', 'band'), may hold values from -3 to 1
Outputs:
- subspace: float32 [384, 384], P('band')
The draws below stay inside these ranges and needn't reach their ends.
All inputs are finite; a program needn't handle non-finite values.
Results may differ from the reference program's by a relative error of at most 0.0003.
Values may be sent and summed in bfloat16 or wider, within the bound.
No kernel may reach another device: no remote copies, remote signals or barrier semaphores. Data moves between devices by JAX's collectives and lax.ppermute only.
A program may use at most 256 MiB of HBM per device.

```python
import math
import jax
import jax.numpy as jnp
from jax import lax

NB = 384
NZ = 64
NX = 48
NY = 96
N_BAND = 16


def mode_angles(key, mode_count):
    wave_key, phase_key = jax.random.split(key, 2)
    wave_numbers = jax.random.randint(wave_key, (NB, mode_count, 3), -2, 3)
    phase_shifts = jax.random.uniform(phase_key, (NB, mode_count), jnp.float32, -math.pi, math.pi)
    first_index = lax.broadcasted_iota(jnp.int32, (1, NX, 1), 1)
    flat_index = lax.broadcasted_iota(jnp.int32, (1, 1, NY * NZ), 2)
    second_index = flat_index // NZ
    third_index = flat_index % NZ
    cell_count = NX * NY * NZ
    angles = []
    for which_mode in range(mode_count):
        first_wave = wave_numbers[:, which_mode, 0][:, None, None]
        second_wave = wave_numbers[:, which_mode, 1][:, None, None]
        third_wave = wave_numbers[:, which_mode, 2][:, None, None]
        tick_count = first_wave * first_index * (NY * NZ) + second_wave * second_index * (NX * NZ) + third_wave * third_index * (NX * NY)
        tick_count = jnp.mod(tick_count, cell_count)
        angle_now = 2.0 * math.pi * tick_count.astype(jnp.float32) / jnp.float32(cell_count)
        angles.append(angle_now + phase_shifts[:, which_mode][:, None, None])
    return angles


def draw_orbitals(key, part):
    key = jax.random.fold_in(key, 11)
    mode_key, weight_key, noise_key = jax.random.split(key, 3)
    angles = mode_angles(mode_key, 3)
    weights = jnp.clip(jax.random.normal(weight_key, (NB, 3), jnp.float32), -2.0, 2.0) / math.sqrt(3.0)
    smooth_part = jnp.zeros((NB, NX, NY * NZ), jnp.float32)
    for which_mode in range(3):
        smooth_part = smooth_part + weights[:, which_mode][:, None, None] * jnp.cos(angles[which_mode])
    noise = jnp.clip(jax.random.normal(noise_key, (NB, NX, NY * NZ), jnp.float32), -4.0, 4.0)
    values = 0.9 * smooth_part + 0.7 * noise
    return values.astype(jnp.bfloat16)


def levels(stream_key, shape, cuts, least, largest):
    level = 1.0
    for axis_at, blocks in cuts:
        heights = jax.random.uniform(jax.random.fold_in(jax.random.fold_in(stream_key, 6), axis_at), (blocks,), jnp.float32, least / len(cuts), largest / len(cuts))
        level = level * jnp.repeat(jnp.exp(heights), shape[axis_at] // blocks).reshape((-1,) + (1,) * (len(shape) - 1 - axis_at))
    return level


def setup_inputs(seed: int = 0) -> dict:
    streams_of = jax.random.split(jax.random.key(seed), 3)
    return {
        "orbitals": draw_orbitals(jax.random.fold_in(streams_of[2], 71), 0),
        "potential": jnp.clip(-3.0 + 4.0 * jax.random.uniform(streams_of[1], (NX, NY * NZ), jnp.float32) ** levels(streams_of[1], (NX, NY * NZ), ((0, 8), (1, 16)), -0.2, 0.2), -3.0, 1.0),
    }


STENCIL = (-5369.0 / 1800.0, 12.0 / 7.0, -15.0 / 56.0, 10.0 / 189.0, -1.0 / 112.0, 2.0 / 1925.0, -1.0 / 16632.0)

def apply_block(block, potential):
    values = block.astype(jnp.float32).reshape(block.shape[0], NX, NY, NZ)
    field = potential.reshape(NX, NY, NZ)
    laplace = 3.0 * STENCIL[0] * values
    for offset in range(1, 7):
        for axis_dim in range(1, 4):
            laplace = laplace + STENCIL[offset] * (jnp.roll(values, offset, axis_dim) + jnp.roll(values, -offset, axis_dim))
    result = -0.5 * laplace + field[None] * values
    return result.reshape(block.shape[0], NX, NY * NZ).astype(jnp.bfloat16)

def reference(orbitals, potential):
    per_block = NB // N_BAND
    blocks = orbitals.reshape(N_BAND, per_block, NX, NY * NZ)
    applied = lax.map(lambda block: apply_block(block, potential), blocks)
    applied = applied.reshape(NB, NX * NY * NZ)
    summed = jnp.dot(orbitals.reshape(NB, NX * NY * NZ), applied.T, preferred_element_type=jnp.float32)
    return summed / jnp.sqrt(jnp.float32(NX * NY * NZ))
```

```python
import functools
import math

import jax
import jax.numpy as jnp
import ml_dtypes
import numpy as np
from jax import lax
from jax.experimental import pallas as pl
from jax.experimental.pallas import tpu as pltpu
from jax.sharding import PartitionSpec as P

NZ = 64
LANES = 128
BLOCKS = 8
WIDTH = LANES // BLOCKS
REACH = 6


STENCIL = (
    -5369.0 / 1800.0,
    12.0 / 7.0,
    -15.0 / 56.0,
    10.0 / 189.0,
    -1.0 / 112.0,
    2.0 / 1925.0,
    -1.0 / 16632.0,
)


def halves(matrix):
    high = matrix.astype(ml_dtypes.bfloat16)
    low = (matrix - high.astype(np.float64)).astype(ml_dtypes.bfloat16)
    return jnp.asarray(np.stack([high, low]))


def upward_plane(cells):
    matrix = np.zeros((2 * cells, cells))
    out = np.arange(cells)
    matrix[out, out] = -0.75 * STENCIL[0]
    for k in range(1, REACH + 1):
        matrix[out + k * NZ, out] += -0.5 * STENCIL[k]
        matrix[out // NZ * NZ + (out + k) % NZ, out] += -0.5 * STENCIL[k]
    return halves(matrix)


def upward_next(layers, rows):
    matrix = np.zeros((3 * LANES, 3 * LANES))
    for x in range(layers):
        for k in range(1, REACH + 1):
            there = x + k - layers
            if 0 <= there < layers:
                for v in range(rows):
                    for j in range(WIDTH):
                        matrix[(there * rows + v) * WIDTH + j, (x * rows + v) * WIDTH + j] = -0.5 * STENCIL[k]
    return halves(matrix)


def spread_matrix():
    matrix = np.zeros((LANES, 3 * LANES), ml_dtypes.bfloat16)
    for piece in range(3):
        for j in range(WIDTH):
            matrix[LANES // 2 + piece * WIDTH + j, j::WIDTH] = 1.0
    return jnp.asarray(matrix)


def exchange_blocks(tiles):
    lane = lax.broadcasted_iota(jnp.int32, tiles[0].shape, 1)
    for bit in (4, 2, 1):
        upper = (lane // (bit * WIDTH)) % 2 == 1
        moved = list(tiles)
        for i in range(BLOCKS):
            if not i & bit:
                a, b = tiles[i], tiles[i | bit]
                moved[i] = jnp.where(upper, pltpu.roll(b, bit * WIDTH, 1), a)
                moved[i | bit] = jnp.where(upper, b, pltpu.roll(a, LANES - bit * WIDTH, 1))
        tiles = moved
    return tiles


def apply_kernel(layers, bands, here_ref, next_ref, plane_ref, potential_ref, out_ref):
    here = here_ref[...]
    both = jnp.concatenate([here, next_ref[...]], axis=1)
    applied = jnp.dot(both, plane_ref[0], preferred_element_type=jnp.float32) + jnp.dot(
        both, plane_ref[1], preferred_element_type=jnp.float32
    )
    center = here.astype(jnp.float32)
    rows = here.shape[1] // LANES
    psi, half = [], []
    for x in range(layers):
        total = applied[x * bands : (x + 1) * bands]
        for k in range(1, layers - x):
            total = total + (-0.5 * STENCIL[k]) * center[(x + k) * bands : (x + k + 1) * bands]
        for v in range(rows):
            psi.append(center[x * bands : (x + 1) * bands, v * LANES : (v + 1) * LANES])
            half.append(total[:, v * LANES : (v + 1) * LANES])
    field = potential_ref[...]
    pieces = []
    for _ in range(3):
        piece = field.astype(jnp.bfloat16).astype(jnp.float32)
        pieces.append(piece)
        field = field - piece
    groups = [psi[:8], psi[8:16], half[:8], half[8:16], psi[16:] + half[16:] + pieces + [jnp.zeros_like(field)]]
    groups = [exchange_blocks(group) for group in groups]
    for there in range(BLOCKS):
        out_ref[there] = jnp.concatenate([group[there] for group in groups], axis=0).astype(jnp.bfloat16)


def product_kernel(bands, scaling, own_ref, blocks_ref, next_plane_ref, spread_ref, out_ref, total, after):
    step = pl.program_id(0)
    count = blocks_ref.shape[0]
    size = count * bands

    def group(at):
        return blocks_ref[:, 0, at * bands : (at + 1) * bands, :].astype(jnp.float32).reshape(size, LANES)

    psi_first, psi_second, rest = group(0), group(1), group(4)
    psi = jnp.concatenate([psi_first, psi_second, rest], axis=1)
    psi_sent = psi.astype(jnp.bfloat16)

    @pl.when(step == 0)
    def _():
        total[...] = jnp.zeros_like(total)

    @pl.when(step > 0)
    def _():
        beyond = jnp.dot(after[...], next_plane_ref[0], preferred_element_type=jnp.float32) + jnp.dot(
            after[...], next_plane_ref[1], preferred_element_type=jnp.float32
        )
        own = blocks_ref[own_ref[0], 0, 4 * bands : 5 * bands, :]
        field = jnp.dot(own, spread_ref[...], preferred_element_type=jnp.float32)
        row = lax.broadcasted_iota(jnp.int32, field.shape, 0)
        lane = lax.broadcasted_iota(jnp.int32, field.shape, 1)
        field = jnp.sum(jnp.where(lane // WIDTH == row, field, 0.0), axis=0, keepdims=True)
        rest_lane = lax.broadcasted_iota(jnp.int32, rest.shape, 1)
        half_rest = jnp.where(rest_lane < 2 * WIDTH, pltpu.roll(rest, LANES - 2 * WIDTH, 1), 0.0)
        half = jnp.concatenate([group(2), group(3), half_rest], axis=1)
        half = half + beyond + (0.5 * field) * psi
        total[...] += lax.dot_general(
            psi_sent, half.astype(jnp.bfloat16), (((1,), (1,)), ((), ())), preferred_element_type=jnp.float32
        )

    after[...] = psi_sent

    @pl.when(step == pl.num_programs(0) - 1)
    def _():
        whole = total[...] * scaling
        out_ref[...] = whole + whole.T


def per_device(orbitals, potential):
    bands, layers, cells_row = orbitals.shape
    count = lax.axis_size("band")
    doms = lax.axis_size("dom")
    cells = cells_row // count
    rows = cells // LANES
    chunk = 5 * bands
    size = count * bands
    cells_all = layers * doms * cells_row
    planes = jnp.transpose(orbitals, (1, 0, 2)).reshape(layers * bands, cells_row)
    field = jnp.pad(potential.reshape(layers * rows, LANES), ((0, bands - layers * rows), (0, 0)))
    packed = pl.pallas_call(
        functools.partial(apply_kernel, layers, bands),
        grid=(count,),
        in_specs=[
            pl.BlockSpec((layers * bands, cells), lambda i: (0, i)),
            pl.BlockSpec((layers * bands, cells), lambda i: (0, (i + 1) % count)),
            pl.BlockSpec((2, 2 * cells, cells), lambda i: (0, 0, 0)),
            pl.BlockSpec((bands, LANES), lambda i: (0, 0)),
        ],
        out_specs=pl.BlockSpec((doms, chunk, LANES), lambda i: (i, 0, 0)),
        out_shape=jax.ShapeDtypeStruct((count * doms, chunk, LANES), jnp.bfloat16),
        compiler_params=pltpu.CompilerParams(vmem_limit_bytes=32 * 2**20),
        name="apply_upward",
    )(planes, planes, upward_plane(cells), field)
    received = lax.all_to_all(packed, ("band", "dom"), 0, 0, tiled=True)
    partial = pl.pallas_call(
        functools.partial(product_kernel, bands, 1.0 / math.sqrt(cells_all)),
        grid=(doms + 1,),
        in_specs=[
            pl.BlockSpec(memory_space=pltpu.SMEM),
            pl.BlockSpec((count, 1, chunk, LANES), lambda i: (0, (doms - i) % doms, 0, 0)),
            pl.BlockSpec((2, 3 * LANES, 3 * LANES), lambda i: (0, 0, 0)),
            pl.BlockSpec((LANES, 3 * LANES), lambda i: (0, 0)),
        ],
        out_specs=pl.BlockSpec((size, size), lambda i: (0, 0)),
        out_shape=jax.ShapeDtypeStruct((size, size), jnp.float32),
        scratch_shapes=[
            pltpu.VMEM((size, size), jnp.float32),
            pltpu.VMEM((size, 3 * LANES), jnp.bfloat16),
        ],
        compiler_params=pltpu.CompilerParams(vmem_limit_bytes=32 * 2**20),
        name="subspace_product",
    )(
        lax.axis_index("band").astype(jnp.int32).reshape(1),
        received.reshape(count, doms, chunk, LANES),
        upward_next(layers, rows),
        spread_matrix(),
    )
    own_rows = lax.all_to_all(partial.reshape(count, bands, size), "band", 0, 0, tiled=True).sum(0)
    copies = jnp.broadcast_to(own_rows, (doms, bands, size))
    return lax.all_to_all(copies, "dom", 0, 0, tiled=True).sum(0)


def solution(mesh):
    placed = (P("band", "dom", None), P("dom", "band"))
    return jax.shard_map(
        per_device, mesh=mesh, in_specs=placed, out_specs=P("band", None), check_vma=False
    )
```

```python
import functools
import math

import jax
import jax.numpy as jnp
import ml_dtypes
import numpy as np
from jax import lax
from jax.experimental import pallas as pl
from jax.experimental.pallas import tpu as pltpu
from jax.sharding import PartitionSpec as P

NZ = 64
LANES = 128
BLOCKS = 8
WIDTH = LANES // BLOCKS
FOLD = 16
REACH = 6


STENCIL = (
    -5369.0 / 1800.0,
    12.0 / 7.0,
    -15.0 / 56.0,
    10.0 / 189.0,
    -1.0 / 112.0,
    2.0 / 1925.0,
    -1.0 / 16632.0,
)


def halves(matrix):
    high = matrix.astype(ml_dtypes.bfloat16)
    low = (matrix - high.astype(np.float64)).astype(ml_dtypes.bfloat16)
    return high, low


def upward_plane():
    matrix = np.zeros((4 * LANES, LANES))
    out = np.arange(LANES)
    matrix[out, out] = -0.75 * STENCIL[0]
    for k in range(1, REACH + 1):
        matrix[out + k * NZ, out] += -0.5 * STENCIL[k]
        matrix[out // NZ * NZ + (out + k) % NZ, out] += -0.5 * STENCIL[k]
    return jnp.asarray(np.concatenate(halves(matrix), axis=1))


def upward_next(layers, rows):
    matrix = np.zeros((2 * LANES, 2 * LANES + 2 * WIDTH))
    for x in range(layers):
        for k in range(1, REACH + 1):
            there = x + k - layers
            for v in range(rows):
                start, end = (there * rows + v) * WIDTH, (x * rows + v) * WIDTH
                if 0 <= there < layers and start < 2 * LANES:
                    for j in range(WIDTH):
                        matrix[start + j, end + j] = -0.5 * STENCIL[k]
    high, low = halves(matrix)
    tail = np.zeros((2 * LANES, LANES - 4 * WIDTH), ml_dtypes.bfloat16)
    return jnp.asarray(np.concatenate([high[:, : 2 * LANES], low[:, : 2 * LANES], high[:, 2 * LANES :], low[:, 2 * LANES :], tail], axis=1))


def exchange_blocks(tiles):
    lane = lax.broadcasted_iota(jnp.int16, tiles[0].shape, 1)
    for bit in (4, 2, 1):
        upper = (lane & (bit * WIDTH)) != 0
        moved = list(tiles)
        for i in range(BLOCKS):
            if not i & bit:
                a, b = tiles[i], tiles[i | bit]
                moved[i] = jnp.where(upper, pltpu.roll(b, bit * WIDTH, 1), a)
                moved[i | bit] = jnp.where(upper, b, pltpu.roll(a, LANES - bit * WIDTH, 1))
        tiles = moved
    return tiles


def coded(potential_ref, rows):
    field = [potential_ref[x : x + 1, v * LANES : (v + 1) * LANES] for x in range(potential_ref.shape[0]) for v in range(rows)]
    field = jnp.concatenate(field + [jnp.zeros((3 * BLOCKS - len(field), LANES), jnp.float32)], axis=0)
    high = jnp.floor(field * 64.0 + 0.5) * (1.0 / 64.0)
    low = field - high
    pairs = jnp.floor(low[8:16] * 1024.0 + 0.5)
    pairs = 17.0 * pltpu.roll(pairs, 4, 0) + pairs
    row = lax.broadcasted_iota(jnp.int32, pairs.shape, 0)
    mixed = jnp.where(row < 2, high[16:], jnp.where(row < 4, pltpu.roll(low[16:], 2, 0), pairs))
    return [high[:8], high[8:16], low[:8], mixed]


def decoded(codes):
    row = lax.broadcasted_iota(jnp.int32, codes.shape, 0)
    block = lax.broadcasted_iota(jnp.int32, codes.shape, 1) >> 4
    parts = []
    for at in range(4):
        part = jnp.where(block == 4 + at, codes, 0.0)
        for shift in (4, 2, 1):
            part = part + pltpu.roll(part, shift * WIDTH, 1)
        parts.append(part)
    first, second, low, mixed = parts
    upper = jnp.floor(mixed * (1.0 / 17.0) + 0.5)
    pairs = jnp.where(row < 4, pltpu.roll(upper, 4, 0), mixed - 17.0 * upper)
    field = [first + low, second + pairs * (1.0 / 1024.0), mixed + pltpu.roll(mixed, 6, 0)]
    return jnp.concatenate([jnp.sum(jnp.where(block == row, part, 0.0), axis=0, keepdims=True) for part in field], axis=1)


def apply_kernel(layers, bands, rows, place_ref, here_ref, next_ref, plane_ref, potential_ref, out_ref):
    here = here_ref[...]
    size = here.shape[0]
    many = here.shape[1] // LANES
    both = jnp.concatenate([here, next_ref[...]], axis=1)
    stacked = jnp.concatenate([both[:, v * LANES : (v + 4) * LANES] for v in range(many)], axis=0)
    applied = jnp.dot(stacked, plane_ref[...], preferred_element_type=jnp.float32)
    applied = applied[:, :LANES] + applied[:, LANES:]
    codes = coded(potential_ref, rows)
    for start in range(0, many, rows):
        psi, half = [], []
        for v in range(start, start + rows):
            center = here[:, v * LANES : (v + 1) * LANES].astype(jnp.float32)
            psi.append([center[x * bands : (x + 1) * bands] for x in range(layers)])
            half.append([])
            for x in range(layers):
                total = applied[v * size + x * bands : v * size + (x + 1) * bands]
                for k in range(1, layers - x):
                    total = total + (-0.5 * STENCIL[k]) * psi[-1][x + k]
                half[-1].append(total)
        psi = [psi[v][x] for x in range(layers) for v in range(rows)]
        half = [half[v][x] for x in range(layers) for v in range(rows)]
        mine = pl.program_id(0) * (many // rows) + start // rows == place_ref[0]
        last = psi[16:] + half[16:]
        last = [part[:FOLD] for part in last] + [jnp.concatenate([part[FOLD:], jnp.where(mine, code, 0.0)], axis=0) for part, code in zip(last, codes)]
        tiles = [
            jnp.concatenate([psi[i], psi[8 + i], half[i], half[8 + i], last[i]], axis=0).astype(jnp.bfloat16)
            for i in range(BLOCKS)
        ]
        for there, tile in enumerate(exchange_blocks(tiles)):
            out_ref[there, start // rows] = tile


def product_kernel(bands, scaling, blocks_ref, next_plane_ref, out_ref, total, after, after_rest, rests):
    step = pl.program_id(0)
    count = blocks_ref.shape[1]
    size = count * bands

    def group(at):
        return blocks_ref[0, :, at * bands : (at + 1) * bands, :].reshape(size, LANES)

    psi = jnp.concatenate([group(0), group(1)], axis=1)
    rest = blocks_ref[0, :, 4 * bands :, :].astype(jnp.float32)
    codes = rest[:, bands - FOLD :]
    beside = pltpu.roll(rest, LANES // 2, 2)[:, : bands - FOLD]
    rest = jnp.concatenate([rest, beside], axis=1).reshape(size, LANES)

    @pl.when(step == 0)
    def _():
        total[...] = jnp.zeros_like(total)

    @pl.when(step > 0)
    def _():
        beyond = jnp.dot(after[...], next_plane_ref[...], preferred_element_type=jnp.float32)
        field = 0.5 * decoded(jnp.sum(codes, axis=0))
        half = jnp.concatenate([group(2), group(3)], axis=1).astype(jnp.float32)
        half = half + beyond[:, : 2 * LANES] + beyond[:, 2 * LANES : 4 * LANES]
        half = half + field[:, : 2 * LANES] * psi.astype(jnp.float32)
        total[...] += lax.dot_general(
            psi, half.astype(jnp.bfloat16), (((1,), (1,)), ((), ())), preferred_element_type=jnp.float32
        )
        beyond_rest = beyond[:, 4 * LANES :]
        beyond_rest = beyond_rest + pltpu.roll(beyond_rest + rest, LANES - 2 * WIDTH, 1)
        beyond_rest = beyond_rest + (-0.5 * STENCIL[REACH]) * after_rest[...] + field[:, 2 * LANES :] * rest
        rests[step - 1, 0] = rest
        rests[step - 1, 1] = beyond_rest

    after[...] = psi
    after_rest[...] = rest

    @pl.when(step == pl.num_programs(0) - 1)
    def _():
        lane = lax.broadcasted_iota(jnp.int32, rest.shape, 1)

        def gathered(which):
            parts = []
            for first in range(0, BLOCKS, 4):
                part = jnp.where(lane < 2 * WIDTH, rests[first, which], 0.0)
                for i in range(1, 4):
                    place = (lane >= 2 * WIDTH * i) & (lane < 2 * WIDTH * (i + 1))
                    part = jnp.where(place, pltpu.roll(rests[first + i, which], 2 * WIDTH * i, 1), part)
                parts.append(part)
            return jnp.concatenate(parts, axis=1).astype(jnp.bfloat16)

        whole = total[...] + lax.dot_general(
            gathered(0), gathered(1), (((1,), (1,)), ((), ())), preferred_element_type=jnp.float32
        )
        whole = whole * scaling
        out_ref[...] = whole + whole.T


def project(bands, scaling, rows, layers, received):
    doms, count, chunk, _ = received.shape
    size = count * bands
    return pl.pallas_call(
        functools.partial(product_kernel, bands, scaling),
        grid=(doms + 1,),
        in_specs=[
            pl.BlockSpec((1, count, chunk, LANES), lambda i: ((doms - i) % doms, 0, 0, 0)),
            pl.BlockSpec((2 * LANES, 5 * LANES), lambda i: (0, 0)),
        ],
        out_specs=pl.BlockSpec((size, size), lambda i: (0, 0)),
        out_shape=jax.ShapeDtypeStruct((size, size), jnp.float32),
        scratch_shapes=[
            pltpu.VMEM((size, size), jnp.float32),
            pltpu.VMEM((size, 2 * LANES), jnp.bfloat16),
            pltpu.VMEM((size, LANES), jnp.float32),
            pltpu.VMEM((doms, 2, size, LANES), jnp.float32),
        ],
        compiler_params=pltpu.CompilerParams(vmem_limit_bytes=24 * 2**20),
        name="subspace_product",
    )(received, pltpu.with_memory_space_constraint(upward_next(layers, rows), pltpu.HBM))


def per_device(orbitals, potential):
    bands, layers, cells_row = orbitals.shape
    count = lax.axis_size("band")
    doms = lax.axis_size("dom")
    cells = cells_row // count
    rows = cells // LANES
    chunk = 4 * bands + FOLD
    size = count * bands
    cells_all = layers * doms * cells_row
    group = 4
    place = lax.axis_index("band").astype(jnp.int32).reshape(1)
    planes = jnp.transpose(orbitals, (1, 0, 2)).reshape(layers * bands, cells_row)
    planes = pltpu.with_memory_space_constraint(planes, pltpu.HBM)
    packed = pl.pallas_call(
        functools.partial(apply_kernel, layers, bands, rows),
        grid=(count // group,),
        in_specs=[
            pl.BlockSpec(memory_space=pltpu.SMEM),
            pl.BlockSpec((layers * bands, group * cells), lambda i: (0, i)),
            pl.BlockSpec((layers * bands, cells), lambda i: (0, (i + 1) * group % count)),
            pl.BlockSpec((4 * LANES, 2 * LANES), lambda i: (0, 0)),
            pl.BlockSpec((layers, cells), lambda i: (0, 0)),
        ],
        out_specs=pl.BlockSpec((doms, group, chunk, LANES), lambda i: (0, i, 0, 0)),
        out_shape=jax.ShapeDtypeStruct((doms, count, chunk, LANES), jnp.bfloat16),
        compiler_params=pltpu.CompilerParams(vmem_limit_bytes=24 * 2**20),
        name="apply_upward",
    )(place, planes, planes, pltpu.with_memory_space_constraint(upward_plane(), pltpu.HBM), potential)
    received = lax.all_to_all(packed.reshape(doms * count, chunk, LANES), ("dom", "band"), 0, 0, tiled=True)
    partial = project(bands, 1.0 / math.sqrt(cells_all), rows, layers, received.reshape(doms, count, chunk, LANES))
    own_rows = lax.all_to_all(partial.reshape(count, bands, size), "band", 0, 0, tiled=True).sum(0)
    copies = jnp.broadcast_to(own_rows, (doms, bands, size))
    return lax.all_to_all(copies, "dom", 0, 0, tiled=True).sum(0)


def solution(mesh):
    placed = (P("band", "dom", None), P("dom", "band"))
    return jax.shard_map(
        per_device, mesh=mesh, in_specs=placed, out_specs=P("band", None), check_vma=False
    )
```

```python
import functools
import math

import jax
import jax.numpy as jnp
import ml_dtypes
import numpy as np
from jax import lax
from jax.experimental import pallas as pl
from jax.experimental.pallas import tpu as pltpu
from jax.sharding import PartitionSpec as P

NZ = 64
LANES = 128
BLOCKS = 8
WIDTH = 8
TALL = 6
REACH = 6
FOLD = 16
WINDOWS = ((-3, -2, -1, 0, 1, 2, 3), (-2, -1, 1, 2, 3, 4), (-1, 2, 3, 4, 5))


STENCIL = (
    -5369.0 / 1800.0,
    12.0 / 7.0,
    -15.0 / 56.0,
    10.0 / 189.0,
    -1.0 / 112.0,
    2.0 / 1925.0,
    -1.0 / 16632.0,
)


def halves(matrix):
    high = matrix.astype(ml_dtypes.bfloat16)
    low = (matrix - high.astype(np.float64)).astype(ml_dtypes.bfloat16)
    return high, low


def sent_plane():
    matrices = []
    for v, window in enumerate(WINDOWS):
        matrix = np.zeros((len(window) * LANES, LANES))
        for out in range(LANES):
            y, z = 2 * v + out // NZ, out % NZ
            for at, other in enumerate(window):
                for half in range(2):
                    there = 2 * other + half
                    k = abs(there - y)
                    if 1 <= k <= REACH and (there > y or there < 0):
                        matrix[at * LANES + half * NZ + z, out] += -0.5 * STENCIL[k]
            start = window.index(v) * LANES + out // NZ * NZ
            for k in range(1, REACH + 1):
                matrix[start + (z + k) % NZ, out] += -0.5 * STENCIL[k]
                if z % WIDTH - k < 0:
                    matrix[start + (z - k) % NZ, out] += -0.5 * STENCIL[k]
        matrices.append(matrix)
    return jnp.asarray(np.concatenate(halves(np.concatenate(matrices)), axis=1))


def placed(x, y, j):
    index = 3 * (x % 3) + y // 2
    half = y % 2 * NZ + j
    return (x // 3, half + index * WIDTH) if index < BLOCKS else (2, half + x // 3 * WIDTH)


def upward_next(layers):
    matrix = np.zeros((2 * LANES, 3 * LANES))
    for x in range(layers):
        for there in range(x + 1):
            for y in range(TALL):
                for j in range(WIDTH):
                    (group, lane), (group_in, lane_in) = placed(x, y, j), placed(there, y, j)
                    if group_in < 2:
                        matrix[group_in * LANES + lane_in, group * LANES + lane] = -0.5 * STENCIL[there + layers - x]
    rest = [np.roll(matrix[:, 2 * LANES :], 2 * WIDTH * i, axis=1) for i in range(4)]
    return tuple(
        jnp.asarray(np.concatenate(halves(each), axis=1)) for each in (matrix[:, : 2 * LANES], np.concatenate(rest))
    )


def upward_block():
    matrix = np.zeros((2 * LANES, LANES))
    rest = np.zeros((LANES, LANES))
    for x in range(3):
        for y in range(TALL):
            for j in range(WIDTH):
                ends = [(x + k, y, j, k) for k in range(1, 3 - x)]
                ends += [(x, y + k, j, k) for k in range(1, TALL - y)]
                ends += [(x, y, j + k, k) for k in range(1, min(REACH, WIDTH - 1 - j) + 1)]
                group, lane = placed(x, y, j)
                for x_in, y_in, j_in, k in ends:
                    group_in, lane_in = placed(x_in, y_in, j_in)
                    if group == 0:
                        matrix[group_in // 2 * LANES + lane_in, lane] = -0.5 * STENCIL[k]
                    else:
                        for block in range(BLOCKS):
                            rest[lane_in + block * WIDTH, lane + block * WIDTH] = -0.5 * STENCIL[k]
    layers = [np.concatenate([matrix[:LANES], np.roll(matrix[LANES:], 2 * WIDTH * i, axis=0)]) for i in range(4)]
    return tuple(jnp.asarray(np.concatenate(halves(each), axis=1)) for each in (np.concatenate(layers), rest))


def exchange_blocks(tiles):
    lane = lax.broadcasted_iota(jnp.int16, tiles[0].shape, 1)
    for bit in (4, 2, 1):
        upper = (lane & (bit * WIDTH)) != 0
        moved = list(tiles)
        for i in range(BLOCKS):
            if not i & bit:
                a, b = tiles[i], tiles[i | bit]
                moved[i] = jnp.where(upper, pltpu.roll(b, bit * WIDTH, 1), a)
                moved[i | bit] = jnp.where(upper, b, pltpu.roll(a, LANES - bit * WIDTH, 1))
        tiles = moved
    return tiles


def coded(potential_ref):
    order = [(x, v) for x in range(6) for v in range(3) if x % 3 + v < 4] + [(2, 2), (5, 2)]
    field = [potential_ref[x : x + 1, v * LANES : (v + 1) * LANES] for x, v in order]
    field = jnp.concatenate(field + [jnp.zeros((3 * BLOCKS - len(field), LANES), jnp.float32)], axis=0)
    pieces = []
    for _ in range(3):
        piece = field.astype(jnp.bfloat16).astype(jnp.float32)
        pieces.append(piece)
        field = field - piece
    high, middle, low = pieces
    mixed = high[16:] + pltpu.roll(middle[16:], 2, 0) + pltpu.roll(low[16:], 4, 0)
    return [high[:16], middle[:16], mixed, low[:8], low[8:16]]


def decoded(codes):
    doms, rows, _ = codes.shape
    codes = codes.reshape(doms * rows, LANES)
    block = (lax.broadcasted_iota(jnp.int32, codes.shape, 1) >> 3) & (BLOCKS - 1)

    def repeated(at):
        part = jnp.where(block == at, codes, 0.0)
        if at:
            part = pltpu.roll(part, LANES - at * WIDTH, 1)
        for shift in (1, 2, 4):
            part = part + pltpu.roll(part, shift * WIDTH, 1)
        return part.reshape(doms, rows, LANES)

    whole = repeated(3) + repeated(7)
    mixed = repeated(4)[:, 8:]
    mixed = mixed + pltpu.roll(mixed, 6, 1) + pltpu.roll(mixed, 4, 1)
    field = [whole[:, :8] + repeated(5)[:, 8:], whole[:, 8:] + repeated(6)[:, 8:], mixed]
    own = lax.broadcasted_iota(jnp.int32, mixed.shape, 1) == (lax.broadcasted_iota(jnp.int32, mixed.shape, 2) >> 3) & (BLOCKS - 1)
    return jnp.concatenate([jnp.sum(jnp.where(own, part, 0.0), axis=1, keepdims=True) for part in field], axis=2)


def apply_kernel(layers, bands, rows, place_ref, before_ref, here_ref, next_ref, plane_ref, potential_ref, out_ref):
    here = here_ref[...]
    size = here.shape[0]
    many = here.shape[1] // LANES
    around = jnp.concatenate([before_ref[...], here, next_ref[...]], axis=1)
    applied, start = [], 0
    for window in WINDOWS:
        stacked = jnp.concatenate(
            [
                jnp.concatenate([around[:, (rows + at + i) * LANES : (rows + at + i + 1) * LANES] for i in window], axis=1)
                for at in range(0, many, rows)
            ],
            axis=0,
        )
        end = start + len(window) * LANES
        part = jnp.dot(stacked, plane_ref[start:end], preferred_element_type=jnp.float32)
        applied.append(part[:, :LANES] + part[:, LANES:])
        start = end
    codes = coded(potential_ref)
    lane = lax.broadcasted_iota(jnp.int32, (bands, LANES), 1)
    for at in range(many // rows):
        psi = [[] for _ in range(layers)]
        sent = [[] for _ in range(layers // 2)]
        lower = ((lane >> 3) & 1) != at % 2
        for v in range(rows):
            center = here[:, (at * rows + v) * LANES : (at * rows + v + 1) * LANES].astype(jnp.float32)
            center = [center[x * bands : (x + 1) * bands] for x in range(layers)]
            total = []
            for x in range(layers):
                part = applied[v][at * size + x * bands : at * size + (x + 1) * bands]
                for other in range(layers):
                    if other > x or (x >= 3 and other < 3):
                        part = part + (-0.5 * STENCIL[abs(other - x)]) * center[other]
                total.append(part)
                psi[x].append(center[x])
            for x in range(layers // 2):
                sent[x].append(jnp.where(lower, total[x], total[x + 3]))
        low, high, sent = sum(psi[:3], []), sum(psi[3:], []), sum(sent, [])
        last = [low[8], high[8], sent[8]]
        last = [each[:FOLD] for each in last] + codes[:1] + [
            jnp.concatenate([each[FOLD:], beside], axis=0) for each, beside in zip(last, codes[2:])
        ] + codes[1:2]
        tiles = [jnp.concatenate([low[i], high[i], sent[i], last[i]], axis=0).astype(jnp.bfloat16) for i in range(BLOCKS)]
        for there, tile in enumerate(exchange_blocks(tiles)):
            out_ref[there, at] = tile


def product_kernel(bands, scaling, place_ref, blocks_ref, *refs):
    matrices, (out_ref, psi_ref, half_ref, psi_rest, sent_rest, field, field_rest), held, arrived = refs[:4], refs[4:11], refs[11:15], refs[15]
    copies = [pltpu.make_async_copy(matrices[i], held[i], arrived.at[i]) for i in range(4)]
    for copy in copies:
        copy.start()
    next_ref, next_rest_ref, block_ref, rest_ref = held
    doms, count = blocks_ref.shape[:2]
    size = count * bands
    even = place_ref[1] == 0
    block = (lax.broadcasted_iota(jnp.int32, (size, LANES), 1) >> 3) & (BLOCKS - 1)
    quads = doms // 4

    def pair(dom):
        return pl.ds(pl.multiple_of(dom * (2 * LANES), 2 * LANES), 2 * LANES)

    field[...] = 0.5 * decoded(blocks_ref[:, place_ref[0], 3 * bands :, :].astype(jnp.float32)) - 0.75 * STENCIL[0]

    @pl.loop(0, doms)
    def _(dom):
        quad, i = dom >> 2, dom & 3
        last = blocks_ref[dom, :, 3 * bands :, :].astype(jnp.float32)
        row = field[dom]
        beside = pltpu.roll(last[:, : bands - FOLD], LANES - 4 * WIDTH, 2)
        last = jnp.concatenate([last, beside], axis=1).reshape(size, LANES)
        mine = block >> 1 == i
        psi_rest[quad] = jnp.where(mine, pltpu.roll(last, 2 * WIDTH * i, 1), psi_rest[quad])
        sent_rest[quad] = jnp.where(mine, pltpu.roll(last, (2 * WIDTH * (i + 7)) & (LANES - 1), 1), sent_rest[quad])
        field_rest[quad] = jnp.where(mine[:1], pltpu.roll(row[:, 2 * LANES :], 2 * WIDTH * i, 1), field_rest[quad])
        psi_ref[:, pair(dom)] = jnp.concatenate(
            [blocks_ref[dom, :, at * bands : (at + 1) * bands, :].reshape(size, LANES) for at in range(2)], axis=1
        )

    for copy in copies:
        copy.wait()

    @pl.loop(0, doms)
    def _(dom):
        i, after = dom & 3, (dom + 1) & (doms - 1)
        psi = psi_ref[:, pair(dom)]
        low, high = psi[:, :LANES], psi[:, LANES:]
        beyond = jnp.dot(psi_ref[:, pair(after)], next_ref[...], preferred_element_type=jnp.float32)
        kept = psi_rest[dom >> 2]
        kept = jnp.where(even, kept, pltpu.roll(kept, LANES - WIDTH, 1)).astype(jnp.bfloat16)
        kept = jnp.concatenate([jnp.where(even, low, high), kept], axis=1)
        rows = pl.ds(pl.multiple_of(i * (2 * LANES), 2 * LANES), 2 * LANES)
        inner = jnp.dot(kept, block_ref[rows, :], preferred_element_type=jnp.float32)
        inner = inner[:, :LANES] + inner[:, LANES:]
        sent = blocks_ref[dom, :, 2 * bands : 3 * bands, :].reshape(size, LANES).astype(jnp.float32)
        lead = psi_rest[after >> 2]
        from_here = 2 * (after & 3)
        lead = pltpu.roll(lead, ((2 - from_here) * WIDTH) & (LANES - 1), 1) * jnp.where(
            block[:1] == 2, -0.5 * STENCIL[5], 0.0
        ) + pltpu.roll(lead, ((5 - from_here) * WIDTH) & (LANES - 1), 1) * jnp.where(block[:1] == 5, -0.5 * STENCIL[4], 0.0)
        row = field[dom]
        half_low = beyond[:, :LANES] + beyond[:, 2 * LANES : 3 * LANES] + jnp.where(even, inner, sent)
        half_low = half_low + row[:, :LANES] * low.astype(jnp.float32)
        half_high = beyond[:, LANES : 2 * LANES] + beyond[:, 3 * LANES :] + jnp.where(even, sent, inner)
        half_high = half_high + lead + row[:, LANES : 2 * LANES] * high.astype(jnp.float32)
        half_ref[:, pair(dom)] = jnp.concatenate([half_low, half_high], axis=1).astype(jnp.bfloat16)

    for quad in range(quads):
        here, other = psi_rest[quad], psi_rest[(quad + 1) % quads]
        beyond = [psi_ref[:, 2 * ((4 * quad + i + 1) % doms) * LANES :][:, : 2 * LANES] for i in range(4)]
        beyond = jnp.dot(jnp.concatenate(beyond, axis=1), next_rest_ref[...], preferred_element_type=jnp.float32)
        ends = here.astype(jnp.bfloat16)
        inner = jnp.dot(ends, rest_ref[...], preferred_element_type=jnp.float32)
        inner = inner[:, :LANES] + inner[:, LANES:]
        after = jnp.where(block >= 6, pltpu.roll(other, 6 * WIDTH, 1), pltpu.roll(here, LANES - 2 * WIDTH, 1))
        half = beyond[:, :LANES] + beyond[:, LANES:] + field_rest[quad] * here + (-0.5 * STENCIL[6]) * after
        half = half + pltpu.roll(after, WIDTH, 1) * jnp.where(block[:1] & 1 == 1, -0.5 * STENCIL[3], 0.0)
        sent = jnp.where(even, pltpu.roll(sent_rest[quad], WIDTH, 1), sent_rest[quad])
        half = half + jnp.where(block & 1 == jnp.where(even, 0, 1), inner, sent)
        place = slice((2 * doms + quad) * LANES, (2 * doms + quad + 1) * LANES)
        psi_ref[:, place] = ends
        half_ref[:, place] = half.astype(jnp.bfloat16)

    whole = lax.dot_general(
        psi_ref[...], half_ref[...], (((1,), (1,)), ((), ())), preferred_element_type=jnp.float32
    )
    whole = whole * scaling
    out_ref[...] = whole + whole.T


def project(bands, scaling, layers, place, received):
    doms, count, chunk, _ = received.shape
    size = count * bands
    width = (2 * doms + doms // 4) * LANES
    whole = pl.BlockSpec(memory_space=pltpu.VMEM)
    matrices = [*upward_next(layers), *upward_block()]
    return pl.pallas_call(
        functools.partial(product_kernel, bands, scaling),
        in_specs=[pl.BlockSpec(memory_space=pltpu.SMEM), whole] + [pl.BlockSpec(memory_space=pl.ANY)] * 4,
        out_specs=whole,
        out_shape=jax.ShapeDtypeStruct((size, size), jnp.float32),
        scratch_shapes=[
            pltpu.VMEM((size, width), jnp.bfloat16),
            pltpu.VMEM((size, width), jnp.bfloat16),
            pltpu.VMEM((doms // 4, size, LANES), jnp.float32),
            pltpu.VMEM((doms // 4, size, LANES), jnp.float32),
            pltpu.VMEM((doms, 1, 3 * LANES), jnp.float32),
            pltpu.VMEM((doms // 4, 1, LANES), jnp.float32),
            *[pltpu.VMEM(each.shape, each.dtype) for each in matrices],
            pltpu.SemaphoreType.DMA((4,)),
        ],
        compiler_params=pltpu.CompilerParams(vmem_limit_bytes=32 * 2**20),
        name="subspace_product",
    )(place, received, *[pltpu.with_memory_space_constraint(each, pltpu.HBM) for each in matrices])


def per_device(orbitals, potential):
    bands, layers, cells_row = orbitals.shape
    count = lax.axis_size("band")
    doms = lax.axis_size("dom")
    cells = cells_row // count
    rows = cells // LANES
    chunk = 3 * bands + FOLD
    size = count * bands
    cells_all = layers * doms * cells_row
    group = 4
    band, dom = lax.axis_index("band"), lax.axis_index("dom")
    place = jnp.stack([band, (band + dom) & 1]).astype(jnp.int32)
    planes = jnp.transpose(orbitals, (1, 0, 2)).reshape(layers * bands, cells_row)
    planes = pltpu.with_memory_space_constraint(planes, pltpu.HBM)
    packed = pl.pallas_call(
        functools.partial(apply_kernel, layers, bands, rows),
        grid=(count // group,),
        in_specs=[
            pl.BlockSpec(memory_space=pltpu.SMEM),
            pl.BlockSpec((layers * bands, cells), lambda i: (0, (i * group + count - 1) % count)),
            pl.BlockSpec((layers * bands, group * cells), lambda i: (0, i)),
            pl.BlockSpec((layers * bands, cells), lambda i: (0, (i + 1) * group % count)),
            pl.BlockSpec((18 * LANES, 2 * LANES), lambda i: (0, 0)),
            pl.BlockSpec((layers, cells), lambda i: (0, 0)),
        ],
        out_specs=pl.BlockSpec((doms, group, chunk, LANES), lambda i: (0, i, 0, 0)),
        out_shape=jax.ShapeDtypeStruct((doms, count, chunk, LANES), jnp.bfloat16),
        compiler_params=pltpu.CompilerParams(vmem_limit_bytes=24 * 2**20),
        name="apply_upward",
    )(
        place,
        planes,
        planes,
        planes,
        pltpu.with_memory_space_constraint(sent_plane(), pltpu.HBM),
        pltpu.with_memory_space_constraint(potential, pltpu.HBM),
    )
    received = lax.all_to_all(packed.reshape(doms * count, chunk, LANES), ("dom", "band"), 0, 0, tiled=True)
    partial = project(bands, 1.0 / math.sqrt(cells_all), layers, place, received.reshape(doms, count, chunk, LANES))
    own_rows = lax.all_to_all(partial.reshape(count, bands, size), "band", 0, 0, tiled=True).sum(0)
    copies = jnp.broadcast_to(own_rows, (doms, bands, size))
    return lax.all_to_all(copies, "dom", 0, 0, tiled=True).sum(0)


def solution(mesh):
    placed = (P("band", "dom", None), P("dom", "band"))
    return jax.shard_map(
        per_device, mesh=mesh, in_specs=placed, out_specs=P("band", None), check_vma=False
    )
```

```python
import functools
import math

import jax
import jax.numpy as jnp
import ml_dtypes
import numpy as np
from jax import lax
from jax.experimental import pallas as pl
from jax.experimental.pallas import tpu as pltpu
from jax.sharding import PartitionSpec as P

NZ = 64
LANES = 128
BLOCKS = 8
WIDTH = 8
TALL = 6
REACH = 6
FOLD = 16
WINDOWS = ((-3, -2, -1, 0, 1, 2, 3), (-2, -1, 1, 2, 3, 4), (-1, 2, 3, 4, 5))


STENCIL = (
    -5369.0 / 1800.0,
    12.0 / 7.0,
    -15.0 / 56.0,
    10.0 / 189.0,
    -1.0 / 112.0,
    2.0 / 1925.0,
    -1.0 / 16632.0,
)


def halves(matrix):
    high = matrix.astype(ml_dtypes.bfloat16)
    low = (matrix - high.astype(np.float64)).astype(ml_dtypes.bfloat16)
    return high, low


def sent_plane():
    matrices = []
    for v, window in enumerate(WINDOWS):
        matrix = np.zeros(((len(window) + 1) * LANES, LANES))
        for out in range(LANES):
            y, z = 2 * v + out // NZ, out % NZ
            for at, other in enumerate(window):
                for half in range(2):
                    there = 2 * other + half
                    k = abs(there - y)
                    if 1 <= k <= REACH and (there > y or there < 0):
                        matrix[at * LANES + half * NZ + z, out] += -0.5 * STENCIL[k]
            own, beside = (at * LANES + out // NZ * NZ for at in (window.index(v), len(window)))
            for k in range(1, REACH + 1):
                matrix[(own if z % WIDTH + k < WIDTH else beside) + (z + k) % NZ, out] += -0.5 * STENCIL[k]
                if z % WIDTH - k < 0:
                    matrix[beside + (z - k) % NZ, out] += -0.5 * STENCIL[k]
        matrices.append(matrix)
    return jnp.asarray(np.concatenate(halves(np.concatenate(matrices)), axis=1))


def placed(x, y, j):
    index = 3 * (x % 3) + y // 2
    half = y % 2 * NZ + j
    return (x // 3, half + index * WIDTH) if index < BLOCKS else (2, half + x // 3 * WIDTH)


def upward_next(layers):
    matrix = np.zeros((2 * LANES, 3 * LANES))
    for x in range(layers):
        for there in range(x + 1):
            for y in range(TALL):
                for j in range(WIDTH):
                    (group, lane), (group_in, lane_in) = placed(x, y, j), placed(there, y, j)
                    if group_in < 2:
                        matrix[group_in * LANES + lane_in, group * LANES + lane] = -0.5 * STENCIL[there + layers - x]
    rest = [np.roll(matrix[:, 2 * LANES :], 2 * WIDTH * i, axis=1) for i in range(4)]
    return tuple(
        jnp.asarray(np.concatenate(halves(each), axis=1)) for each in (matrix[:, : 2 * LANES], np.concatenate(rest))
    )


def upward_block():
    matrix = np.zeros((2 * LANES, LANES))
    rest = np.zeros((LANES, LANES))
    for x in range(3):
        for y in range(TALL):
            for j in range(WIDTH):
                ends = [(x + k, y, j, k) for k in range(1, 3 - x)]
                ends += [(x, y + k, j, k) for k in range(1, TALL - y)]
                ends += [(x, y, j + k, k) for k in range(1, min(REACH, WIDTH - 1 - j) + 1)]
                group, lane = placed(x, y, j)
                for x_in, y_in, j_in, k in ends:
                    group_in, lane_in = placed(x_in, y_in, j_in)
                    if group == 0:
                        matrix[group_in // 2 * LANES + lane_in, lane] = -0.5 * STENCIL[k]
                    else:
                        for block in range(BLOCKS):
                            rest[lane_in + block * WIDTH, lane + block * WIDTH] = -0.5 * STENCIL[k]
    layers = [np.concatenate([matrix[:LANES], np.roll(matrix[LANES:], 2 * WIDTH * i, axis=0)]) for i in range(4)]
    return tuple(jnp.asarray(np.concatenate(halves(each), axis=1)) for each in (np.concatenate(layers), rest))


def exchange_blocks(tiles):
    lane = lax.broadcasted_iota(jnp.int16, tiles[0].shape, 1)
    for bit in (4, 2, 1):
        upper = (lane & (bit * WIDTH)) != 0
        moved = list(tiles)
        for i in range(BLOCKS):
            if not i & bit:
                a, b = tiles[i], tiles[i | bit]
                moved[i] = jnp.where(upper, pltpu.roll(b, bit * WIDTH, 1), a)
                moved[i | bit] = jnp.where(upper, b, pltpu.roll(a, LANES - bit * WIDTH, 1))
        tiles = moved
    return tiles


def coded(potential_ref):
    order = [(x, v) for x in range(6) for v in range(3) if x % 3 + v < 4] + [(2, 2), (5, 2)]
    field = [potential_ref[x : x + 1, v * LANES : (v + 1) * LANES] for x, v in order]
    field = jnp.concatenate(field + [jnp.zeros((3 * BLOCKS - len(field), LANES), jnp.float32)], axis=0)
    pieces = []
    for _ in range(3):
        piece = field.astype(jnp.bfloat16).astype(jnp.float32)
        pieces.append(piece)
        field = field - piece
    high, middle, low = pieces
    mixed = high[16:] + pltpu.roll(middle[16:], 2, 0) + pltpu.roll(low[16:], 4, 0)
    return [high[:16], middle[:16], mixed, low[:8], low[8:16]]


def decoded(codes):
    doms, rows, _ = codes.shape
    codes = codes.reshape(doms * rows, LANES)
    block = (lax.broadcasted_iota(jnp.int32, codes.shape, 1) >> 3) & (BLOCKS - 1)

    def repeated(at):
        part = jnp.where(block == at, codes, 0.0)
        if at:
            part = pltpu.roll(part, LANES - at * WIDTH, 1)
        for shift in (1, 2, 4):
            part = part + pltpu.roll(part, shift * WIDTH, 1)
        return part.reshape(doms, rows, LANES)

    whole = repeated(3) + repeated(7)
    mixed = repeated(4)[:, 8:]
    mixed = mixed + pltpu.roll(mixed, 6, 1) + pltpu.roll(mixed, 4, 1)
    field = [whole[:, :8] + repeated(5)[:, 8:], whole[:, 8:] + repeated(6)[:, 8:], mixed]
    own = lax.broadcasted_iota(jnp.int32, mixed.shape, 1) == (lax.broadcasted_iota(jnp.int32, mixed.shape, 2) >> 3) & (BLOCKS - 1)
    return jnp.concatenate([jnp.sum(jnp.where(own, part, 0.0), axis=1, keepdims=True) for part in field], axis=2)


def apply_kernel(layers, bands, rows, group, place_ref, planes_ref, plane_ref, potential_ref, out_ref, held, plane, potential, arrived):
    size, width = planes_ref.shape
    side, part = rows * LANES, width // 4
    ends = [(width - side, 0, side)] + [(i * part, side + i * part, part) for i in range(4)] + [(0, side + width, side)]
    copies = [
        pltpu.make_async_copy(planes_ref.at[:, pl.ds(start, count)], held.at[:, pl.ds(end, count)], arrived.at[i])
        for i, (start, end, count) in enumerate(ends)
    ]
    copies += [pltpu.make_async_copy(plane_ref, plane, arrived.at[6]), pltpu.make_async_copy(potential_ref, potential, arrived.at[7])]
    for i in (7, 0, 1, 6, 2, 3, 4, 5):
        copies[i].start()
    for i in (7, 0, 1, 6):
        copies[i].wait()
    codes = coded(potential)
    lane = lax.broadcasted_iota(jnp.int32, (BLOCKS, LANES), 1)
    steps = width // (group * side)

    @pl.loop(0, steps)
    def _(step):
        for i in range(2, 6):

            @pl.when(step == (i - 1) * steps // 4 - 1)
            def _():
                copies[i].wait()

        around = held[:, pl.ds(pl.multiple_of(step * (group * side), side), (group + 2) * side)]
        low, high, even, odd = [], [], [], []
        blank = jnp.zeros((-3 * bands % 16, LANES), jnp.float32)
        lower = (lane[:1] >> 3) & 1 == 0
        for v in range((group + 2) * rows):
            center = around[:, v * LANES : (v + 1) * LANES].astype(jnp.float32)
            low.append(center[: 3 * bands])
            high.append(center[3 * bands :])
            odd.append(jnp.where(lower, low[v], high[v]))
            even.append(jnp.where(lower, high[v], low[v]))
        layered = [even, odd]
        spaced = [[jnp.concatenate([each, blank], axis=0).astype(jnp.bfloat16) for each in which] for which in layered]
        applied, start = [], 0
        for v, window in enumerate(WINDOWS):
            stacked = jnp.concatenate(
                [
                    jnp.concatenate(
                        [spaced[at % 2][rows * (at + 1) + i] for i in window] + [spaced[1 - at % 2][rows * (at + 1) + v]], axis=1
                    )
                    for at in range(group)
                ],
                axis=0,
            )
            end = start + (len(window) + 1) * LANES
            applied.append(jnp.dot(stacked, plane[start:end], preferred_element_type=jnp.float32))
            start = end
        taller = spaced[0][0].shape[0]
        weight = {k: -0.5 * STENCIL[k] for k in range(1, 4)}
        for at in range(group):
            mine, others = layered[at % 2], layered[1 - at % 2]
            first = lower if at % 2 else ~lower
            across = {i: jnp.where(first, -0.5 * STENCIL[3 + i], -0.5 * STENCIL[3 - i]) for i in range(-2, 3)}
            sent = [[], [], []]
            psi = [[] for _ in range(layers)]
            for v in range(rows):
                place = rows * (at + 1) + v
                for x in range(3):
                    slices = [slice(other * bands, (other + 1) * bands) for other in range(3)]
                    total = applied[v][at * taller :][slices[x]]
                    total = total[:, :LANES] + total[:, LANES:]
                    for other in range(3):
                        if other > x:
                            total = total + weight[other - x] * mine[place][slices[other]]
                        total = total + across[other - x] * others[place][slices[other]]
                    sent[x].append(total)
                    psi[x].append(low[place][slices[x]])
                    psi[x + 3].append(high[place][slices[x]])
            first, second, sent = sum(psi[:3], []), sum(psi[3:], []), sum(sent, [])
            last = [first[8], second[8], sent[8]]
            last = [each[:FOLD] for each in last] + codes[:1] + [
                jnp.concatenate([each[FOLD:], beside], axis=0) for each, beside in zip(last, codes[2:])
            ] + codes[1:2]
            tiles = [jnp.concatenate([first[i], second[i], sent[i], last[i]], axis=0).astype(jnp.bfloat16) for i in range(BLOCKS)]
            for there, tile in enumerate(exchange_blocks(tiles)):
                out_ref[there, step * group + at] = tile


def product_kernel(bands, scaling, place_ref, blocks_ref, *refs):
    matrices, (kept_ref, given_ref, out_ref, psi_ref, half_ref, psi_rest, sent_rest, field, field_rest) = refs[:4], refs[4:13]
    held, arrived = refs[13:17], refs[17]
    copies = [pltpu.make_async_copy(matrices[i], held[i], arrived.at[i]) for i in range(4)]
    for copy in copies:
        copy.start()
    next_ref, next_rest_ref, block_ref, rest_ref = held
    doms, count = blocks_ref.shape[:2]
    size = count * bands
    even = place_ref[1] == 0
    block = (lax.broadcasted_iota(jnp.int32, (size, LANES), 1) >> 3) & (BLOCKS - 1)
    quads = doms // 4

    def pair(dom):
        return pl.ds(pl.multiple_of(dom * (2 * LANES), 2 * LANES), 2 * LANES)

    field[...] = 0.5 * decoded(blocks_ref[:, place_ref[0], 3 * bands :, :].astype(jnp.float32)) - 0.75 * STENCIL[0]

    @pl.loop(0, doms, unroll=2)
    def _(dom):
        quad, i = dom >> 2, dom & 3
        last = blocks_ref[dom, :, 3 * bands :, :].astype(jnp.float32)
        row = field[dom]
        beside = pltpu.roll(last[:, : bands - FOLD], LANES - 4 * WIDTH, 2)
        last = jnp.concatenate([last, beside], axis=1).reshape(size, LANES)
        mine = block >> 1 == i
        psi_rest[quad] = jnp.where(mine, pltpu.roll(last, 2 * WIDTH * i, 1), psi_rest[quad])
        sent_rest[quad] = jnp.where(mine, pltpu.roll(last, (2 * WIDTH * (i + 7)) & (LANES - 1), 1), sent_rest[quad])
        field_rest[quad] = jnp.where(mine[:1], pltpu.roll(row[:, 2 * LANES :], 2 * WIDTH * i, 1), field_rest[quad])
        psi_ref[:, pair(dom)] = jnp.concatenate(
            [blocks_ref[dom, :, at * bands : (at + 1) * bands, :].reshape(size, LANES) for at in range(2)], axis=1
        )

    for copy in copies:
        copy.wait()

    @pl.loop(0, doms, unroll=2)
    def _(dom):
        i, after = dom & 3, (dom + 1) & (doms - 1)
        psi = psi_ref[:, pair(dom)]
        low, high = psi[:, :LANES], psi[:, LANES:]
        beyond = jnp.dot(psi_ref[:, pair(after)], next_ref[...], preferred_element_type=jnp.float32)
        kept = psi_rest[dom >> 2]
        kept = jnp.where(even, kept, pltpu.roll(kept, LANES - WIDTH, 1)).astype(jnp.bfloat16)
        kept = jnp.concatenate([jnp.where(even, low, high), kept], axis=1)
        rows = pl.ds(pl.multiple_of(i * (2 * LANES), 2 * LANES), 2 * LANES)
        inner = jnp.dot(kept, block_ref[rows, :], preferred_element_type=jnp.float32)
        inner = inner[:, :LANES] + inner[:, LANES:]
        sent = blocks_ref[dom, :, 2 * bands : 3 * bands, :].reshape(size, LANES).astype(jnp.float32)
        lead = psi_rest[after >> 2]
        from_here = 2 * (after & 3)
        lead = pltpu.roll(lead, ((2 - from_here) * WIDTH) & (LANES - 1), 1) * jnp.where(
            block[:1] == 2, -0.5 * STENCIL[5], 0.0
        ) + pltpu.roll(lead, ((5 - from_here) * WIDTH) & (LANES - 1), 1) * jnp.where(block[:1] == 5, -0.5 * STENCIL[4], 0.0)
        row = field[dom]
        half_low = beyond[:, :LANES] + beyond[:, 2 * LANES : 3 * LANES] + jnp.where(even, inner, sent)
        half_low = half_low + row[:, :LANES] * low.astype(jnp.float32)
        half_high = beyond[:, LANES : 2 * LANES] + beyond[:, 3 * LANES :] + jnp.where(even, sent, inner)
        half_high = half_high + lead + row[:, LANES : 2 * LANES] * high.astype(jnp.float32)
        half_ref[:, pair(dom)] = jnp.concatenate([half_low, half_high], axis=1).astype(jnp.bfloat16)

    for quad in range(quads):
        here, other = psi_rest[quad], psi_rest[(quad + 1) % quads]
        beyond = [psi_ref[:, 2 * ((4 * quad + i + 1) % doms) * LANES :][:, : 2 * LANES] for i in range(4)]
        beyond = jnp.dot(jnp.concatenate(beyond, axis=1), next_rest_ref[...], preferred_element_type=jnp.float32)
        ends = here.astype(jnp.bfloat16)
        inner = jnp.dot(ends, rest_ref[...], preferred_element_type=jnp.float32)
        inner = inner[:, :LANES] + inner[:, LANES:]
        after = jnp.where(block >= 6, pltpu.roll(other, 6 * WIDTH, 1), pltpu.roll(here, LANES - 2 * WIDTH, 1))
        half = beyond[:, :LANES] + beyond[:, LANES:] + field_rest[quad] * here + (-0.5 * STENCIL[6]) * after
        half = half + pltpu.roll(after, WIDTH, 1) * jnp.where(block[:1] & 1 == 1, -0.5 * STENCIL[3], 0.0)
        sent = jnp.where(even, pltpu.roll(sent_rest[quad], WIDTH, 1), sent_rest[quad])
        half = half + jnp.where(block & 1 == jnp.where(even, 0, 1), inner, sent)
        place = slice((2 * doms + quad) * LANES, (2 * doms + quad + 1) * LANES)
        psi_ref[:, place] = ends
        half_ref[:, place] = half.astype(jnp.bfloat16)

    whole = lax.dot_general(
        psi_ref[...], half_ref[...], (((1,), (1,)), ((), ())), preferred_element_type=jnp.float32
    )
    whole = whole * scaling
    whole = whole + whole.T
    core = place_ref[0] & 1
    for pair in range(count // 2):
        for which in range(2):
            rows = whole[(2 * pair + which) * bands : (2 * pair + which + 1) * bands]
            out_ref[which, pair] = rows
    first, second = out_ref[0], out_ref[1]
    kept_ref[...] = jnp.where(core == 0, first, second)
    given_ref[...] = jnp.where(core == 0, second, first)


def project(bands, scaling, layers, place, received):
    doms, count, chunk, _ = received.shape
    size = count * bands
    width = (2 * doms + doms // 4) * LANES
    whole = pl.BlockSpec(memory_space=pltpu.VMEM)
    matrices = [*upward_next(layers), *upward_block()]
    return pl.pallas_call(
        functools.partial(product_kernel, bands, scaling),
        in_specs=[pl.BlockSpec(memory_space=pltpu.SMEM), whole] + [pl.BlockSpec(memory_space=pl.ANY)] * 4,
        out_specs=[whole] * 2,
        out_shape=[jax.ShapeDtypeStruct((count // 2, bands, size), jnp.float32)] * 2,
        scratch_shapes=[
            pltpu.VMEM((2, count // 2, bands, size), jnp.float32),
            pltpu.VMEM((size, width), jnp.bfloat16),
            pltpu.VMEM((size, width), jnp.bfloat16),
            pltpu.VMEM((doms // 4, size, LANES), jnp.float32),
            pltpu.VMEM((doms // 4, size, LANES), jnp.float32),
            pltpu.VMEM((doms, 1, 3 * LANES), jnp.float32),
            pltpu.VMEM((doms // 4, 1, LANES), jnp.float32),
            *[pltpu.VMEM(each.shape, each.dtype) for each in matrices],
            pltpu.SemaphoreType.DMA((4,)),
        ],
        compiler_params=pltpu.CompilerParams(vmem_limit_bytes=32 * 2**20),
        name="subspace_product",
    )(place, received, *[pltpu.with_memory_space_constraint(each, pltpu.HBM) for each in matrices])


def pack(doms, count, place, orbitals, potential):
    bands, layers, cells_row = orbitals.shape
    cells = cells_row // count
    rows = cells // LANES
    chunk = 3 * bands + FOLD
    group = 4
    planes = jnp.transpose(orbitals, (1, 0, 2)).reshape(layers * bands, cells_row)
    operands = [pltpu.with_memory_space_constraint(each, pltpu.HBM) for each in (planes, sent_plane(), potential)]
    return pl.pallas_call(
        functools.partial(apply_kernel, layers, bands, rows, group),
        in_specs=[pl.BlockSpec(memory_space=pltpu.SMEM)] + [pl.BlockSpec(memory_space=pl.ANY)] * 3,
        out_specs=pl.BlockSpec(memory_space=pltpu.VMEM),
        out_shape=jax.ShapeDtypeStruct((doms, count, chunk, LANES), jnp.bfloat16),
        scratch_shapes=[
            pltpu.VMEM((layers * bands, cells_row + 2 * cells), jnp.bfloat16),
            pltpu.VMEM((21 * LANES, 2 * LANES), jnp.bfloat16),
            pltpu.VMEM(potential.shape, jnp.float32),
            pltpu.SemaphoreType.DMA((8,)),
        ],
        compiler_params=pltpu.CompilerParams(vmem_limit_bytes=24 * 2**20),
        name="apply_upward",
    )(place, *operands)


def per_device(orbitals, potential):
    bands, layers, cells_row = orbitals.shape
    count = lax.axis_size("band")
    doms = lax.axis_size("dom")
    size = count * bands
    cells_all = layers * doms * cells_row
    band, dom = lax.axis_index("band"), lax.axis_index("dom")
    place = jnp.stack([band, (band + dom) & 1]).astype(jnp.int32)
    packed = pack(doms, count, place, orbitals, potential)
    chunk = packed.shape[2]
    received = lax.all_to_all(packed.reshape(doms * count, chunk, LANES), ("dom", "band"), 0, 0, tiled=True)
    kept, given = project(bands, 1.0 / math.sqrt(cells_all), layers, place, received.reshape(doms, count, chunk, LANES))
    cores = [(i, i ^ 1) for i in range(count)]
    same_core = [list(range(core, count, 2)) for core in range(2)]
    kept = kept + lax.ppermute(given, "band", cores)
    own_rows = lax.all_to_all(kept, "band", 0, 0, axis_index_groups=same_core, tiled=True).sum(0)
    copies = jnp.broadcast_to(own_rows, (doms, bands, size))
    return lax.all_to_all(copies, "dom", 0, 0, tiled=True).sum(0)


def solution(mesh):
    placed = (P("band", "dom", None), P("dom", "band"))
    return jax.shard_map(
        per_device, mesh=mesh, in_specs=placed, out_specs=P("band", None), check_vma=False
    )
```

```python
import functools
import math

import jax
import jax.numpy as jnp
import ml_dtypes
import numpy as np
from jax import lax
from jax.experimental import pallas as pl
from jax.experimental.pallas import tpu as pltpu
from jax.sharding import PartitionSpec as P

NZ = 64
LANES = 128
BLOCKS = 8
WIDTH = 8
TALL = 6
REACH = 6
FOLD = 16
WINDOWS = ((-3, -2, -1, 0, 1, 2, 3), (-2, -1, 1, 2, 3, 4), (-1, 2, 3, 4, 5))


STENCIL = (
    -5369.0 / 1800.0,
    12.0 / 7.0,
    -15.0 / 56.0,
    10.0 / 189.0,
    -1.0 / 112.0,
    2.0 / 1925.0,
    -1.0 / 16632.0,
)


def halves(matrix):
    high = matrix.astype(ml_dtypes.bfloat16)
    low = (matrix - high.astype(np.float64)).astype(ml_dtypes.bfloat16)
    return high, low


def sent_plane():
    matrices = []
    for v, window in enumerate(WINDOWS):
        matrix = np.zeros(((len(window) + 1) * LANES, LANES))
        for out in range(LANES):
            y, z = 2 * v + out // NZ, out % NZ
            for at, other in enumerate(window):
                for half in range(2):
                    there = 2 * other + half
                    k = abs(there - y)
                    if 1 <= k <= REACH and (there > y or there < 0):
                        matrix[at * LANES + half * NZ + z, out] += -0.5 * STENCIL[k]
            own, beside = (at * LANES + out // NZ * NZ for at in (window.index(v), len(window)))
            for k in range(1, REACH + 1):
                matrix[(own if z % WIDTH + k < WIDTH else beside) + (z + k) % NZ, out] += -0.5 * STENCIL[k]
                if z % WIDTH - k < 0:
                    matrix[beside + (z - k) % NZ, out] += -0.5 * STENCIL[k]
        matrices.append(matrix)
    return jnp.asarray(np.concatenate(halves(np.concatenate(matrices)), axis=1))


def placed(x, y, j):
    index = 3 * (x % 3) + y // 2
    half = y % 2 * NZ + j
    return (x // 3, half + index * WIDTH) if index < BLOCKS else (2, half + x // 3 * WIDTH)


def upward_next(layers):
    matrix = np.zeros((2 * LANES, 3 * LANES))
    for x in range(layers):
        for there in range(x + 1):
            for y in range(TALL):
                for j in range(WIDTH):
                    (group, lane), (group_in, lane_in) = placed(x, y, j), placed(there, y, j)
                    if group_in < 2:
                        matrix[group_in * LANES + lane_in, group * LANES + lane] = -0.5 * STENCIL[there + layers - x]
    rest = [np.roll(matrix[:, 2 * LANES :], 2 * WIDTH * i, axis=1) for i in range(4)]
    return tuple(
        turned(np.concatenate(halves(each), axis=1)) for each in (matrix[:, : 2 * LANES], np.concatenate(rest))
    )


def upward_block():
    matrix = np.zeros((2 * LANES, LANES))
    rest = np.zeros((LANES, LANES))
    for x in range(3):
        for y in range(TALL):
            for j in range(WIDTH):
                ends = [(x + k, y, j, k) for k in range(1, 3 - x)]
                ends += [(x, y + k, j, k) for k in range(1, TALL - y)]
                ends += [(x, y, j + k, k) for k in range(1, min(REACH, WIDTH - 1 - j) + 1)]
                group, lane = placed(x, y, j)
                for x_in, y_in, j_in, k in ends:
                    group_in, lane_in = placed(x_in, y_in, j_in)
                    if group == 0:
                        matrix[group_in // 2 * LANES + lane_in, lane] = -0.5 * STENCIL[k]
                    else:
                        for block in range(BLOCKS):
                            rest[lane_in + block * WIDTH, lane + block * WIDTH] = -0.5 * STENCIL[k]
    layers = [np.concatenate([matrix[:LANES], np.roll(matrix[LANES:], 2 * WIDTH * i, axis=0)]) for i in range(4)]
    return tuple(turned(np.concatenate(halves(each), axis=1)) for each in (np.concatenate(layers), rest))


def exchange_blocks(tiles):
    lane = lax.broadcasted_iota(jnp.int16, tiles[0].shape, 1)
    tiles = [pltpu.roll(tile, i * WIDTH, 1) if i else tile for i, tile in enumerate(tiles)]
    for bit in (1, 2, 4):
        upper = (lane & (bit * WIDTH)) != 0
        tiles = [jnp.where(upper, tiles[(i + bit) % BLOCKS], tiles[i]) for i in range(BLOCKS)]
    return [tiles[-c % BLOCKS] for c in range(BLOCKS)]


def turned(matrix):
    rows, columns = matrix.shape
    tiles = matrix.reshape(rows // LANES, LANES, columns // LANES, LANES)
    return jnp.asarray(np.stack([np.roll(tiles, (c * WIDTH, c * WIDTH), (1, 3)).reshape(rows, columns) for c in range(BLOCKS)]))


def coded(potential_ref):
    order = [(x, v) for x in range(6) for v in range(3) if x % 3 + v < 4] + [(2, 2), (5, 2)]
    field = [potential_ref[x : x + 1, v * LANES : (v + 1) * LANES] for x, v in order]
    field = jnp.concatenate(field + [jnp.zeros((3 * BLOCKS - len(field), LANES), jnp.float32)], axis=0)
    pieces = []
    for _ in range(3):
        piece = field.astype(jnp.bfloat16).astype(jnp.float32)
        pieces.append(piece)
        field = field - piece
    high, middle, low = pieces
    mixed = high[16:] + pltpu.roll(middle[16:], 2, 0) + pltpu.roll(low[16:], 4, 0)
    return [high[:16], middle[:16], mixed, low[:8], low[8:16]]


def decoded(codes, block):
    doms, rows, _ = codes.shape
    codes = codes.reshape(doms * rows, LANES)
    block = block[: doms * rows]

    def repeated(at):
        part = jnp.where(block == at, codes, 0.0)
        if at:
            part = pltpu.roll(part, LANES - at * WIDTH, 1)
        for shift in (1, 2, 4):
            part = part + pltpu.roll(part, shift * WIDTH, 1)
        return part.reshape(doms, rows, LANES)

    whole = repeated(3) + repeated(7)
    mixed = repeated(4)[:, 8:]
    mixed = mixed + pltpu.roll(mixed, 6, 1) + pltpu.roll(mixed, 4, 1)
    field = [whole[:, :8] + repeated(5)[:, 8:], whole[:, 8:] + repeated(6)[:, 8:], mixed]
    own = lax.broadcasted_iota(jnp.int32, mixed.shape, 1) == block[: doms * BLOCKS].reshape(mixed.shape)
    return jnp.concatenate([jnp.sum(jnp.where(own, part, 0.0), axis=1, keepdims=True) for part in field], axis=2)


def apply_kernel(layers, bands, rows, group, place_ref, planes_ref, plane_ref, potential_ref, out_ref, held, plane, potential, spaced, arrived):
    size, width = planes_ref.shape
    side, part = rows * LANES, width // 4
    ends = [(width - side, 0, side)] + [(i * part, side + i * part, part) for i in range(4)] + [(0, side + width, side)]
    copies = [
        pltpu.make_async_copy(planes_ref.at[:, pl.ds(start, count)], held.at[:, pl.ds(end, count)], arrived.at[i])
        for i, (start, end, count) in enumerate(ends)
    ]
    copies += [pltpu.make_async_copy(plane_ref, plane, arrived.at[6]), pltpu.make_async_copy(potential_ref, potential, arrived.at[7])]
    for i in (7, 0, 1, 6, 2, 3, 4, 5):
        copies[i].start()
    for i in (7, 0, 1, 6):
        copies[i].wait()
    codes = coded(potential)
    lane = lax.broadcasted_iota(jnp.int32, (BLOCKS, LANES), 1)
    steps = width // (group * side)

    @pl.loop(0, steps)
    def _(step):
        for i in range(2, 6):

            @pl.when(step == (i - 1) * steps // 4 - 1)
            def _():
                copies[i].wait()

        base = step * (group * side)
        blank = jnp.zeros((-3 * bands % 16, LANES), jnp.float32)
        lower = (lane[:1] >> 3) & 1 == 0

        def layered(v):
            center = held[:, pl.ds(pl.multiple_of(base + v * LANES, LANES), LANES)].astype(jnp.float32)
            return center[: 3 * bands], center[3 * bands :]

        for v in range((group + 2) * rows):
            low, high = layered(v)
            for which, upper in ((0, low), (1, high)):
                each = jnp.where(lower, high if which == 0 else low, upper)
                spaced[which, :, v * LANES : (v + 1) * LANES] = jnp.concatenate([each, blank], axis=0).astype(jnp.bfloat16)
        applied, start = [], 0
        for v, window in enumerate(WINDOWS):
            stacked = jnp.concatenate(
                [
                    jnp.concatenate(
                        [spaced[at % 2, :, (rows * (at + 1) + i) * LANES : (rows * (at + 1) + i + 1) * LANES] for i in window]
                        + [spaced[1 - at % 2, :, (rows * (at + 1) + v) * LANES : (rows * (at + 1) + v + 1) * LANES]],
                        axis=1,
                    )
                    for at in range(group)
                ],
                axis=0,
            )
            end = start + (len(window) + 1) * LANES
            applied.append(jnp.dot(stacked, plane[start:end], preferred_element_type=jnp.float32))
            start = end
        taller = spaced.shape[1]
        weight = {k: -0.5 * STENCIL[k] for k in range(1, 4)}
        for at in range(group):
            first = lower if at % 2 else ~lower
            across = {i: jnp.where(first, -0.5 * STENCIL[3 + i], -0.5 * STENCIL[3 - i]) for i in range(-2, 3)}
            sent = [[], [], []]
            psi = [[] for _ in range(layers)]
            for v in range(rows):
                place = rows * (at + 1) + v
                low, high = layered(place)
                mine = jnp.where(first, low, high)
                others = jnp.where(first, high, low)
                for x in range(3):
                    slices = [slice(other * bands, (other + 1) * bands) for other in range(3)]
                    total = applied[v][at * taller :][slices[x]]
                    total = total[:, :LANES] + total[:, LANES:]
                    for other in range(3):
                        if other > x:
                            total = total + weight[other - x] * mine[slices[other]]
                        total = total + across[other - x] * others[slices[other]]
                    sent[x].append(total)
                    psi[x].append(low[slices[x]])
                    psi[x + 3].append(high[slices[x]])
            low, high, sent = sum(psi[:3], []), sum(psi[3:], []), sum(sent, [])
            last = [low[8], high[8], sent[8]]
            last = [each[:FOLD] for each in last] + codes[:1] + [
                jnp.concatenate([each[FOLD:], beside], axis=0) for each, beside in zip(last, codes[2:])
            ] + codes[1:2]
            tiles = [jnp.concatenate([low[i], high[i], sent[i], last[i]], axis=0).astype(jnp.bfloat16) for i in range(BLOCKS)]
            for there, tile in enumerate(exchange_blocks(tiles)):
                out_ref[there, step * group + at] = tile


def product_kernel(bands, scaling, place_ref, blocks_ref, *refs):
    matrices, (kept_ref, given_ref, out_ref, psi_ref, half_ref, psi_rest, sent_rest, field, field_rest) = refs[:4], refs[4:13]
    held, arrived = refs[13:17], refs[17]
    copies = [pltpu.make_async_copy(matrices[i].at[place_ref[2]], held[i], arrived.at[i]) for i in range(4)]
    for copy in copies:
        copy.start()
    next_ref, next_rest_ref, block_ref, rest_ref = held
    doms, count = blocks_ref.shape[:2]
    size = count * bands
    even = place_ref[1] == 0
    block = ((lax.broadcasted_iota(jnp.int32, (size, LANES), 1) >> 3) - place_ref[2]) & (BLOCKS - 1)
    quads = doms // 4

    def pair(dom):
        return pl.ds(pl.multiple_of(dom * (2 * LANES), 2 * LANES), 2 * LANES)

    field[...] = 0.5 * decoded(blocks_ref[:, place_ref[0], 3 * bands :, :].astype(jnp.float32), block) - 0.75 * STENCIL[0]

    @pl.loop(0, doms, unroll=2)
    def _(dom):
        quad, i = dom >> 2, dom & 3
        last = blocks_ref[dom, :, 3 * bands :, :].astype(jnp.float32)
        row = field[dom]
        beside = pltpu.roll(last[:, : bands - FOLD], LANES - 4 * WIDTH, 2)
        last = jnp.concatenate([last, beside], axis=1).reshape(size, LANES)
        mine = block >> 1 == i
        psi_rest[quad] = jnp.where(mine, pltpu.roll(last, 2 * WIDTH * i, 1), psi_rest[quad])
        sent_rest[quad] = jnp.where(mine, pltpu.roll(last, (2 * WIDTH * (i + 7)) & (LANES - 1), 1), sent_rest[quad])
        field_rest[quad] = jnp.where(mine[:1], pltpu.roll(row[:, 2 * LANES :], 2 * WIDTH * i, 1), field_rest[quad])
        psi_ref[:, pair(dom)] = jnp.concatenate(
            [blocks_ref[dom, :, at * bands : (at + 1) * bands, :].reshape(size, LANES) for at in range(2)], axis=1
        )

    for copy in copies:
        copy.wait()

    @pl.loop(0, doms, unroll=2)
    def _(dom):
        i, after = dom & 3, (dom + 1) & (doms - 1)
        psi = psi_ref[:, pair(dom)]
        low, high = psi[:, :LANES], psi[:, LANES:]
        beyond = jnp.dot(psi_ref[:, pair(after)], next_ref[...], preferred_element_type=jnp.float32)
        kept = psi_rest[dom >> 2]
        kept = jnp.where(even, kept, pltpu.roll(kept, LANES - WIDTH, 1)).astype(jnp.bfloat16)
        kept = jnp.concatenate([jnp.where(even, low, high), kept], axis=1)
        rows = pl.ds(pl.multiple_of(i * (2 * LANES), 2 * LANES), 2 * LANES)
        inner = jnp.dot(kept, block_ref[rows, :], preferred_element_type=jnp.float32)
        inner = inner[:, :LANES] + inner[:, LANES:]
        sent = blocks_ref[dom, :, 2 * bands : 3 * bands, :].reshape(size, LANES).astype(jnp.float32)
        lead = psi_rest[after >> 2]
        from_here = 2 * (after & 3)
        lead = pltpu.roll(lead, ((2 - from_here) * WIDTH) & (LANES - 1), 1) * jnp.where(
            block[:1] == 2, -0.5 * STENCIL[5], 0.0
        ) + pltpu.roll(lead, ((5 - from_here) * WIDTH) & (LANES - 1), 1) * jnp.where(block[:1] == 5, -0.5 * STENCIL[4], 0.0)
        row = field[dom]
        half_low = beyond[:, :LANES] + beyond[:, 2 * LANES : 3 * LANES] + jnp.where(even, inner, sent)
        half_low = half_low + row[:, :LANES] * low.astype(jnp.float32)
        half_high = beyond[:, LANES : 2 * LANES] + beyond[:, 3 * LANES :] + jnp.where(even, sent, inner)
        half_high = half_high + lead + row[:, LANES : 2 * LANES] * high.astype(jnp.float32)
        half_ref[:, pair(dom)] = jnp.concatenate([half_low, half_high], axis=1).astype(jnp.bfloat16)

    for quad in range(quads):
        here, other = psi_rest[quad], psi_rest[(quad + 1) % quads]
        beyond = [psi_ref[:, 2 * ((4 * quad + i + 1) % doms) * LANES :][:, : 2 * LANES] for i in range(4)]
        beyond = jnp.dot(jnp.concatenate(beyond, axis=1), next_rest_ref[...], preferred_element_type=jnp.float32)
        ends = here.astype(jnp.bfloat16)
        inner = jnp.dot(ends, rest_ref[...], preferred_element_type=jnp.float32)
        inner = inner[:, :LANES] + inner[:, LANES:]
        after = jnp.where(block >= 6, pltpu.roll(other, 6 * WIDTH, 1), pltpu.roll(here, LANES - 2 * WIDTH, 1))
        half = beyond[:, :LANES] + beyond[:, LANES:] + field_rest[quad] * here + (-0.5 * STENCIL[6]) * after
        half = half + pltpu.roll(after, WIDTH, 1) * jnp.where(block[:1] & 1 == 1, -0.5 * STENCIL[3], 0.0)
        sent = jnp.where(even, pltpu.roll(sent_rest[quad], WIDTH, 1), sent_rest[quad])
        half = half + jnp.where(block & 1 == jnp.where(even, 0, 1), inner, sent)
        place = slice((2 * doms + quad) * LANES, (2 * doms + quad + 1) * LANES)
        psi_ref[:, place] = ends
        half_ref[:, place] = half.astype(jnp.bfloat16)

    whole = lax.dot_general(
        psi_ref[...], half_ref[...], (((1,), (1,)), ((), ())), preferred_element_type=jnp.float32
    )
    whole = whole * scaling
    whole = whole + whole.T
    core = place_ref[0] & 1
    for pair in range(count // 2):
        for which in range(2):
            rows = whole[(2 * pair + which) * bands : (2 * pair + which + 1) * bands]
            out_ref[which, pair] = rows
    first, second = out_ref[0], out_ref[1]
    kept_ref[...] = jnp.where(core == 0, first, second)
    given_ref[...] = jnp.where(core == 0, second, first)


def project(bands, scaling, layers, place, received):
    doms, count, chunk, _ = received.shape
    size = count * bands
    width = (2 * doms + doms // 4) * LANES
    whole = pl.BlockSpec(memory_space=pltpu.VMEM)
    matrices = [*upward_next(layers), *upward_block()]
    return pl.pallas_call(
        functools.partial(product_kernel, bands, scaling),
        in_specs=[pl.BlockSpec(memory_space=pltpu.SMEM), whole] + [pl.BlockSpec(memory_space=pl.ANY)] * 4,
        out_specs=[whole] * 2,
        out_shape=[jax.ShapeDtypeStruct((count // 2, bands, size), jnp.float32)] * 2,
        scratch_shapes=[
            pltpu.VMEM((2, count // 2, bands, size), jnp.float32),
            pltpu.VMEM((size, width), jnp.bfloat16),
            pltpu.VMEM((size, width), jnp.bfloat16),
            pltpu.VMEM((doms // 4, size, LANES), jnp.float32),
            pltpu.VMEM((doms // 4, size, LANES), jnp.float32),
            pltpu.VMEM((doms, 1, 3 * LANES), jnp.float32),
            pltpu.VMEM((doms // 4, 1, LANES), jnp.float32),
            *[pltpu.VMEM(each.shape[1:], each.dtype) for each in matrices],
            pltpu.SemaphoreType.DMA((4,)),
        ],
        compiler_params=pltpu.CompilerParams(vmem_limit_bytes=32 * 2**20),
        name="subspace_product",
    )(place, received, *[pltpu.with_memory_space_constraint(each, pltpu.HBM) for each in matrices])


def pack(doms, count, place, orbitals, potential):
    bands, layers, cells_row = orbitals.shape
    cells = cells_row // count
    rows = cells // LANES
    chunk = 3 * bands + FOLD
    group = 4
    planes = jnp.transpose(orbitals, (1, 0, 2)).reshape(layers * bands, cells_row)
    operands = [pltpu.with_memory_space_constraint(each, pltpu.HBM) for each in (planes, sent_plane(), potential)]
    return pl.pallas_call(
        functools.partial(apply_kernel, layers, bands, rows, group),
        in_specs=[pl.BlockSpec(memory_space=pltpu.SMEM)] + [pl.BlockSpec(memory_space=pl.ANY)] * 3,
        out_specs=pl.BlockSpec(memory_space=pltpu.VMEM),
        out_shape=jax.ShapeDtypeStruct((doms, count, chunk, LANES), jnp.bfloat16),
        scratch_shapes=[
            pltpu.VMEM((layers * bands, cells_row + 2 * cells), jnp.bfloat16),
            pltpu.VMEM((21 * LANES, 2 * LANES), jnp.bfloat16),
            pltpu.VMEM(potential.shape, jnp.float32),
            pltpu.VMEM((2, 3 * bands + -3 * bands % 16, (group + 2) * cells), jnp.bfloat16),
            pltpu.SemaphoreType.DMA((8,)),
        ],
        compiler_params=pltpu.CompilerParams(vmem_limit_bytes=24 * 2**20),
        name="apply_upward",
    )(place, *operands)


def per_device(orbitals, potential):
    bands, layers, cells_row = orbitals.shape
    count = lax.axis_size("band")
    doms = lax.axis_size("dom")
    size = count * bands
    cells_all = layers * doms * cells_row
    band, dom = lax.axis_index("band"), lax.axis_index("dom")
    place = jnp.stack([band, (band + dom) & 1, dom]).astype(jnp.int32)
    packed = pack(doms, count, place, orbitals, potential)
    chunk = packed.shape[2]
    received = lax.all_to_all(packed.reshape(doms * count, chunk, LANES), ("dom", "band"), 0, 0, tiled=True)
    kept, given = project(bands, 1.0 / math.sqrt(cells_all), layers, place, received.reshape(doms, count, chunk, LANES))
    cores = [(i, i ^ 1) for i in range(count)]
    same_core = [list(range(core, count, 2)) for core in range(2)]
    kept = kept + lax.ppermute(given, "band", cores)
    own_rows = lax.all_to_all(kept, "band", 0, 0, axis_index_groups=same_core, tiled=True).sum(0)
    copies = jnp.broadcast_to(own_rows, (doms, bands, size))
    return lax.all_to_all(copies, "dom", 0, 0, tiled=True).sum(0)


def solution(mesh):
    placed = (P("band", "dom", None), P("dom", "band"))
    return jax.shard_map(
        per_device, mesh=mesh, in_specs=placed, out_specs=P("band", None), check_vma=False
    )
```

```python
import functools
import math

import jax
import jax.numpy as jnp
import ml_dtypes
import numpy as np
from jax import lax
from jax.experimental import pallas as pl
from jax.experimental.pallas import tpu as pltpu
from jax.sharding import PartitionSpec as P

NZ = 64
LANES = 128
BLOCKS = 8
WIDTH = 8
TALL = 6
REACH = 6
FOLD = 16
WINDOWS = ((-3, -2, -1, 0, 1, 2, 3), (-2, -1, 1, 2, 3, 4), (-1, 2, 3, 4, 5))


STENCIL = (
    -5369.0 / 1800.0,
    12.0 / 7.0,
    -15.0 / 56.0,
    10.0 / 189.0,
    -1.0 / 112.0,
    2.0 / 1925.0,
    -1.0 / 16632.0,
)


def halves(matrix):
    high = matrix.astype(ml_dtypes.bfloat16)
    low = (matrix - high.astype(np.float64)).astype(ml_dtypes.bfloat16)
    return high, low


def sent_plane(plane_ref):
    row = lax.broadcasted_iota(jnp.int32, (LANES, LANES), 0)
    lane = lax.broadcasted_iota(jnp.int32, (LANES, LANES), 1)
    apart = (row - lane) & (NZ - 1)
    same_half = (row ^ lane) & NZ == 0
    same_block = (row ^ lane) & (NZ - WIDTH) == 0
    parts = [[float(part) for part in halves(np.float64(-0.5 * c))] for c in STENCIL]
    start = 0
    for which in range(2):
        along = jnp.zeros((LANES, LANES), jnp.float32)
        for k in range(1, REACH + 1):
            along = jnp.where((apart == k) | (apart == NZ - k), parts[k][which], along)
        along = jnp.where(same_half, along, 0.0)
        inside = jnp.where(same_block & (row > lane), along, 0.0)
        outside = jnp.where(same_block, 0.0, along)
        columns = slice(which * LANES, (which + 1) * LANES)
        start = 0
        for v, window in enumerate(WINDOWS):
            for other in window:
                tile = []
                for half in range(2):
                    weight = []
                    for out in range(2):
                        there, y = 2 * other + half, 2 * v + out
                        k = abs(there - y)
                        weight.append(parts[k][which] if 1 <= k <= REACH and (there > y or there < 0) else 0.0)
                    above = slice(half * NZ, (half + 1) * NZ)
                    across = jnp.where(lane[above] < NZ, weight[0], weight[1])
                    part = jnp.where(apart[above] == 0, across, 0.0)
                    tile.append(part + inside[above] if other == v else part)
                plane_ref[start : start + LANES, columns] = jnp.concatenate(tile, axis=0).astype(jnp.bfloat16)
                start += LANES
            plane_ref[start : start + LANES, columns] = outside.astype(jnp.bfloat16)
            start += LANES


def placed(x, y, j):
    index = 3 * (x % 3) + y // 2
    half = y % 2 * NZ + j
    return (x // 3, half + index * WIDTH) if index < BLOCKS else (2, half + x // 3 * WIDTH)


def upward_next(layers):
    matrix = np.zeros((2 * LANES, 3 * LANES))
    for x in range(layers):
        for there in range(x + 1):
            for y in range(TALL):
                for j in range(WIDTH):
                    (group, lane), (group_in, lane_in) = placed(x, y, j), placed(there, y, j)
                    if group_in < 2:
                        matrix[group_in * LANES + lane_in, group * LANES + lane] = -0.5 * STENCIL[there + layers - x]
    rest = [np.roll(matrix[:, 2 * LANES :], 2 * WIDTH * i, axis=1) for i in range(4)]
    return tuple(
        turned(np.concatenate(halves(each), axis=1)) for each in (matrix[:, : 2 * LANES], np.concatenate(rest))
    )


def upward_block():
    matrix = np.zeros((2 * LANES, LANES))
    rest = np.zeros((LANES, LANES))
    for x in range(3):
        for y in range(TALL):
            for j in range(WIDTH):
                ends = [(x + k, y, j, k) for k in range(1, 3 - x)]
                ends += [(x, y + k, j, k) for k in range(1, TALL - y)]
                ends += [(x, y, j + k, k) for k in range(1, min(REACH, WIDTH - 1 - j) + 1)]
                group, lane = placed(x, y, j)
                for x_in, y_in, j_in, k in ends:
                    group_in, lane_in = placed(x_in, y_in, j_in)
                    if group == 0:
                        matrix[group_in // 2 * LANES + lane_in, lane] = -0.5 * STENCIL[k]
                    else:
                        for block in range(BLOCKS):
                            rest[lane_in + block * WIDTH, lane + block * WIDTH] = -0.5 * STENCIL[k]
    layers = [np.concatenate([matrix[:LANES], np.roll(matrix[LANES:], 2 * WIDTH * i, axis=0)]) for i in range(4)]
    return tuple(turned(np.concatenate(halves(each), axis=1)) for each in (np.concatenate(layers), rest))


def exchange_blocks(tiles):
    lane = lax.broadcasted_iota(jnp.int16, tiles[0].shape, 1)
    tiles = [pltpu.roll(tile, i * WIDTH, 1) if i else tile for i, tile in enumerate(tiles)]
    for bit in (1, 2, 4):
        upper = (lane & (bit * WIDTH)) != 0
        tiles = [jnp.where(upper, tiles[(i + bit) % BLOCKS], tiles[i]) for i in range(BLOCKS)]
    return [tiles[-c % BLOCKS] for c in range(BLOCKS)]


def turned(matrix):
    rows, columns = matrix.shape
    tiles = matrix.reshape(rows // LANES, LANES, columns // LANES, LANES)
    return jnp.asarray(np.stack([np.roll(tiles, (c * WIDTH, c * WIDTH), (1, 3)).reshape(rows, columns) for c in range(BLOCKS)]))


def coded(potential_ref):
    order = [(x, v) for x in range(6) for v in range(3) if x % 3 + v < 4] + [(2, 2), (5, 2)]
    field = [potential_ref[x : x + 1, v * LANES : (v + 1) * LANES] for x, v in order]
    field = jnp.concatenate(field + [jnp.zeros((3 * BLOCKS - len(field), LANES), jnp.float32)], axis=0)
    pieces = []
    for _ in range(3):
        piece = field.astype(jnp.bfloat16).astype(jnp.float32)
        pieces.append(piece)
        field = field - piece
    high, middle, low = pieces
    mixed = high[16:] + pltpu.roll(middle[16:], 2, 0) + pltpu.roll(low[16:], 4, 0)
    return [high[:16], middle[:16], mixed, low[:8], low[8:16]]


def decoded(codes, block):
    doms, rows, _ = codes.shape
    codes = codes.reshape(doms * rows, LANES)
    block = block[: doms * rows]

    def repeated(at):
        part = jnp.where(block == at, codes, 0.0)
        if at:
            part = pltpu.roll(part, LANES - at * WIDTH, 1)
        for shift in (1, 2, 4):
            part = part + pltpu.roll(part, shift * WIDTH, 1)
        return part.reshape(doms, rows, LANES)

    whole = repeated(3) + repeated(7)
    mixed = repeated(4)[:, 8:]
    mixed = mixed + pltpu.roll(mixed, 6, 1) + pltpu.roll(mixed, 4, 1)
    field = [whole[:, :8] + repeated(5)[:, 8:], whole[:, 8:] + repeated(6)[:, 8:], mixed]
    own = lax.broadcasted_iota(jnp.int32, mixed.shape, 1) == block[: doms * BLOCKS].reshape(mixed.shape)
    return jnp.concatenate([jnp.sum(jnp.where(own, part, 0.0), axis=1, keepdims=True) for part in field], axis=2)


def apply_kernel(layers, bands, rows, group, place_ref, planes_ref, potential_ref, out_ref, held, plane, potential, spaced, arrived):
    size, width = planes_ref.shape
    side, part = rows * LANES, width // 4
    ends = [(width - side, 0, side)] + [(i * part, side + i * part, part) for i in range(4)] + [(0, side + width, side)]
    copies = [
        pltpu.make_async_copy(planes_ref.at[:, pl.ds(start, count)], held.at[:, pl.ds(end, count)], arrived.at[i])
        for i, (start, end, count) in enumerate(ends)
    ]
    copies.append(pltpu.make_async_copy(potential_ref, potential, arrived.at[6]))
    for i in (6, 0, 1, 2, 3, 4, 5):
        copies[i].start()
    sent_plane(plane)
    for i in (6, 0, 1):
        copies[i].wait()
    codes = coded(potential)
    lane = lax.broadcasted_iota(jnp.int32, (BLOCKS, LANES), 1)
    steps = width // (group * side)

    @pl.loop(0, steps)
    def _(step):
        for i in range(2, 6):

            @pl.when(step == (i - 1) * steps // 4 - 1)
            def _():
                copies[i].wait()

        base = step * (group * side)
        blank = jnp.zeros((-3 * bands % 16, LANES), jnp.float32)
        lower = (lane[:1] >> 3) & 1 == 0

        def layered(v):
            center = held[:, pl.ds(pl.multiple_of(base + v * LANES, LANES), LANES)].astype(jnp.float32)
            return center[: 3 * bands], center[3 * bands :]

        for v in range((group + 2) * rows):
            low, high = layered(v)
            for which, upper in ((0, low), (1, high)):
                each = jnp.where(lower, high if which == 0 else low, upper)
                spaced[which, :, v * LANES : (v + 1) * LANES] = jnp.concatenate([each, blank], axis=0).astype(jnp.bfloat16)
        applied, start = [], 0
        for v, window in enumerate(WINDOWS):
            stacked = jnp.concatenate(
                [
                    jnp.concatenate(
                        [spaced[at % 2, :, (rows * (at + 1) + i) * LANES : (rows * (at + 1) + i + 1) * LANES] for i in window]
                        + [spaced[1 - at % 2, :, (rows * (at + 1) + v) * LANES : (rows * (at + 1) + v + 1) * LANES]],
                        axis=1,
                    )
                    for at in range(group)
                ],
                axis=0,
            )
            end = start + (len(window) + 1) * LANES
            applied.append(jnp.dot(stacked, plane[start:end], preferred_element_type=jnp.float32))
            start = end
        taller = spaced.shape[1]
        weight = {k: -0.5 * STENCIL[k] for k in range(1, 4)}
        for at in range(group):
            first = lower if at % 2 else ~lower
            across = {i: jnp.where(first, -0.5 * STENCIL[3 + i], -0.5 * STENCIL[3 - i]) for i in range(-2, 3)}
            sent = [[], [], []]
            psi = [[] for _ in range(layers)]
            for v in range(rows):
                place = rows * (at + 1) + v
                low, high = layered(place)
                mine = jnp.where(first, low, high)
                others = jnp.where(first, high, low)
                for x in range(3):
                    slices = [slice(other * bands, (other + 1) * bands) for other in range(3)]
                    total = applied[v][at * taller :][slices[x]]
                    total = total[:, :LANES] + total[:, LANES:]
                    for other in range(3):
                        if other > x:
                            total = total + weight[other - x] * mine[slices[other]]
                        total = total + across[other - x] * others[slices[other]]
                    sent[x].append(total)
                    psi[x].append(low[slices[x]])
                    psi[x + 3].append(high[slices[x]])
            low, high, sent = sum(psi[:3], []), sum(psi[3:], []), sum(sent, [])
            last = [low[8], high[8], sent[8]]
            last = [each[:FOLD] for each in last] + codes[:1] + [
                jnp.concatenate([each[FOLD:], beside], axis=0) for each, beside in zip(last, codes[2:])
            ] + codes[1:2]
            tiles = [jnp.concatenate([low[i], high[i], sent[i], last[i]], axis=0).astype(jnp.bfloat16) for i in range(BLOCKS)]
            for there, tile in enumerate(exchange_blocks(tiles)):
                out_ref[there, step * group + at] = tile


def product_kernel(bands, scaling, place_ref, blocks_ref, *refs):
    matrices, (kept_ref, given_ref, out_ref, psi_ref, half_ref, psi_rest, sent_rest, field, field_rest) = refs[:4], refs[4:13]
    held, arrived = refs[13:17], refs[17]
    copies = [pltpu.make_async_copy(matrices[i].at[place_ref[2]], held[i], arrived.at[i]) for i in range(4)]
    for copy in copies:
        copy.start()
    next_ref, next_rest_ref, block_ref, rest_ref = held
    doms, count = blocks_ref.shape[:2]
    size = count * bands
    even = place_ref[1] == 0
    block = ((lax.broadcasted_iota(jnp.int32, (size, LANES), 1) >> 3) - place_ref[2]) & (BLOCKS - 1)
    quads = doms // 4
    block_short = block.astype(jnp.int16)

    def pair(dom):
        return pl.ds(pl.multiple_of(dom * (2 * LANES), 2 * LANES), 2 * LANES)

    field[...] = 0.5 * decoded(blocks_ref[:, place_ref[0], 3 * bands :, :].astype(jnp.float32), block) - 0.75 * STENCIL[0]

    @pl.loop(0, doms, unroll=2)
    def _(dom):
        quad, i = dom >> 2, dom & 3
        last = blocks_ref[dom, :, 3 * bands :, :].astype(jnp.float32)
        row = field[dom]
        beside = pltpu.roll(last[:, : bands - FOLD], LANES - 4 * WIDTH, 2)
        last = jnp.concatenate([last, beside], axis=1).reshape(size, LANES).astype(jnp.bfloat16)
        mine = block_short & 6 == (2 * i).astype(jnp.int16)
        psi_rest[quad] = jnp.where(mine, pltpu.roll(last, 2 * WIDTH * i, 1), psi_rest[quad])
        sent_rest[quad] = jnp.where(mine, pltpu.roll(last, (2 * WIDTH * (i + 7)) & (LANES - 1), 1), sent_rest[quad])
        field_rest[quad] = jnp.where(block[:1] >> 1 == i, pltpu.roll(row[:, 2 * LANES :], 2 * WIDTH * i, 1), field_rest[quad])
        psi_ref[:, pair(dom)] = jnp.concatenate(
            [blocks_ref[dom, :, at * bands : (at + 1) * bands, :].reshape(size, LANES) for at in range(2)], axis=1
        )

    for copy in copies:
        copy.wait()

    @pl.loop(0, doms, unroll=2)
    def _(dom):
        i, after = dom & 3, (dom + 1) & (doms - 1)
        psi = psi_ref[:, pair(dom)]
        low, high = psi[:, :LANES], psi[:, LANES:]
        beyond = jnp.dot(psi_ref[:, pair(after)], next_ref[...], preferred_element_type=jnp.float32)
        kept = psi_rest[dom >> 2]
        kept = jnp.where(even, kept, pltpu.roll(kept, LANES - WIDTH, 1))
        kept = jnp.concatenate([jnp.where(even, low, high), kept], axis=1)
        rows = pl.ds(pl.multiple_of(i * (2 * LANES), 2 * LANES), 2 * LANES)
        inner = jnp.dot(kept, block_ref[rows, :], preferred_element_type=jnp.float32)
        inner = inner[:, :LANES] + inner[:, LANES:]
        sent = blocks_ref[dom, :, 2 * bands : 3 * bands, :].reshape(size, LANES).astype(jnp.float32)
        lead = psi_rest[after >> 2]
        from_here = 2 * (after & 3)
        lead = [pltpu.roll(lead, ((place - from_here) * WIDTH) & (LANES - 1), 1).astype(jnp.float32) for place in (2, 5)]
        lead = lead[0] * jnp.where(block[:1] == 2, -0.5 * STENCIL[5], 0.0) + lead[1] * jnp.where(block[:1] == 5, -0.5 * STENCIL[4], 0.0)
        row = field[dom]
        half_low = beyond[:, :LANES] + beyond[:, 2 * LANES : 3 * LANES] + jnp.where(even, inner, sent)
        half_low = half_low + row[:, :LANES] * low.astype(jnp.float32)
        half_high = beyond[:, LANES : 2 * LANES] + beyond[:, 3 * LANES :] + jnp.where(even, sent, inner)
        half_high = half_high + lead + row[:, LANES : 2 * LANES] * high.astype(jnp.float32)
        half_ref[:, pair(dom)] = jnp.concatenate([half_low, half_high], axis=1).astype(jnp.bfloat16)

    for quad in range(quads):
        here, other = psi_rest[quad], psi_rest[(quad + 1) % quads]
        beyond = [psi_ref[:, 2 * ((4 * quad + i + 1) % doms) * LANES :][:, : 2 * LANES] for i in range(4)]
        beyond = jnp.dot(jnp.concatenate(beyond, axis=1), next_rest_ref[...], preferred_element_type=jnp.float32)
        inner = jnp.dot(here, rest_ref[...], preferred_element_type=jnp.float32)
        inner = inner[:, :LANES] + inner[:, LANES:]
        after = jnp.where(block_short >= 6, pltpu.roll(other, 6 * WIDTH, 1), pltpu.roll(here, LANES - 2 * WIDTH, 1))
        half = beyond[:, :LANES] + beyond[:, LANES:] + field_rest[quad] * here.astype(jnp.float32)
        half = half + (-0.5 * STENCIL[6]) * after.astype(jnp.float32)
        half = half + pltpu.roll(after, WIDTH, 1).astype(jnp.float32) * jnp.where(block[:1] & 1 == 1, -0.5 * STENCIL[3], 0.0)
        sent = jnp.where(even, pltpu.roll(sent_rest[quad], WIDTH, 1), sent_rest[quad]).astype(jnp.float32)
        half = half + jnp.where(block & 1 == jnp.where(even, 0, 1), inner, sent)
        place = slice((2 * doms + quad) * LANES, (2 * doms + quad + 1) * LANES)
        psi_ref[:, place] = here
        half_ref[:, place] = half.astype(jnp.bfloat16)

    whole = lax.dot_general(
        psi_ref[...], half_ref[...], (((1,), (1,)), ((), ())), preferred_element_type=jnp.float32
    )
    whole = whole * scaling
    whole = whole + whole.T
    core = place_ref[0] & 1
    for pair in range(count // 2):
        for which in range(2):
            rows = whole[(2 * pair + which) * bands : (2 * pair + which + 1) * bands]
            out_ref[which, pair] = rows
    first, second = out_ref[0], out_ref[1]
    kept_ref[...] = jnp.where(core == 0, first, second)
    given_ref[...] = jnp.where(core == 0, second, first)


def project(bands, scaling, layers, place, received):
    doms, count, chunk, _ = received.shape
    size = count * bands
    width = (2 * doms + doms // 4) * LANES
    whole = pl.BlockSpec(memory_space=pltpu.VMEM)
    matrices = [*upward_next(layers), *upward_block()]
    return pl.pallas_call(
        functools.partial(product_kernel, bands, scaling),
        in_specs=[pl.BlockSpec(memory_space=pltpu.SMEM), whole] + [pl.BlockSpec(memory_space=pl.ANY)] * 4,
        out_specs=[whole] * 2,
        out_shape=[jax.ShapeDtypeStruct((count // 2, bands, size), jnp.float32)] * 2,
        scratch_shapes=[
            pltpu.VMEM((2, count // 2, bands, size), jnp.float32),
            pltpu.VMEM((size, width), jnp.bfloat16),
            pltpu.VMEM((size, width), jnp.bfloat16),
            pltpu.VMEM((doms // 4, size, LANES), jnp.bfloat16),
            pltpu.VMEM((doms // 4, size, LANES), jnp.bfloat16),
            pltpu.VMEM((doms, 1, 3 * LANES), jnp.float32),
            pltpu.VMEM((doms // 4, 1, LANES), jnp.float32),
            *[pltpu.VMEM(each.shape[1:], each.dtype) for each in matrices],
            pltpu.SemaphoreType.DMA((4,)),
        ],
        compiler_params=pltpu.CompilerParams(vmem_limit_bytes=32 * 2**20),
        name="subspace_product",
    )(place, received, *[pltpu.with_memory_space_constraint(each, pltpu.HBM) for each in matrices])


def pack(doms, count, place, orbitals, potential):
    bands, layers, cells_row = orbitals.shape
    cells = cells_row // count
    rows = cells // LANES
    chunk = 3 * bands + FOLD
    group = 4
    planes = jnp.transpose(orbitals, (1, 0, 2)).reshape(layers * bands, cells_row)
    operands = [pltpu.with_memory_space_constraint(each, pltpu.HBM) for each in (planes, potential)]
    return pl.pallas_call(
        functools.partial(apply_kernel, layers, bands, rows, group),
        in_specs=[pl.BlockSpec(memory_space=pltpu.SMEM)] + [pl.BlockSpec(memory_space=pl.ANY)] * 2,
        out_specs=pl.BlockSpec(memory_space=pltpu.VMEM),
        out_shape=jax.ShapeDtypeStruct((doms, count, chunk, LANES), jnp.bfloat16),
        scratch_shapes=[
            pltpu.VMEM((layers * bands, cells_row + 2 * cells), jnp.bfloat16),
            pltpu.VMEM((21 * LANES, 2 * LANES), jnp.bfloat16),
            pltpu.VMEM(potential.shape, jnp.float32),
            pltpu.VMEM((2, 3 * bands + -3 * bands % 16, (group + 2) * cells), jnp.bfloat16),
            pltpu.SemaphoreType.DMA((7,)),
        ],
        compiler_params=pltpu.CompilerParams(vmem_limit_bytes=24 * 2**20),
        name="apply_upward",
    )(place, *operands)


def per_device(orbitals, potential):
    bands, layers, cells_row = orbitals.shape
    count = lax.axis_size("band")
    doms = lax.axis_size("dom")
    size = count * bands
    cells_all = layers * doms * cells_row
    band, dom = lax.axis_index("band"), lax.axis_index("dom")
    place = jnp.stack([band, (band + dom) & 1, dom]).astype(jnp.int32)
    packed = pack(doms, count, place, orbitals, potential)
    chunk = packed.shape[2]
    received = lax.all_to_all(packed.reshape(doms * count, chunk, LANES), ("dom", "band"), 0, 0, tiled=True)
    kept, given = project(bands, 1.0 / math.sqrt(cells_all), layers, place, received.reshape(doms, count, chunk, LANES))
    cores = [(i, i ^ 1) for i in range(count)]
    same_core = [list(range(core, count, 2)) for core in range(2)]
    kept = kept + lax.ppermute(given, "band", cores)
    own_rows = lax.all_to_all(kept, "band", 0, 0, axis_index_groups=same_core, tiled=True).sum(0)
    copies = jnp.broadcast_to(own_rows, (doms, bands, size))
    return lax.all_to_all(copies, "dom", 0, 0, tiled=True).sum(0)


def solution(mesh):
    placed = (P("band", "dom", None), P("dom", "band"))
    return jax.shard_map(
        per_device, mesh=mesh, in_specs=placed, out_specs=P("band", None), check_vma=False
    )
```

```python
import functools
import math

import jax
import jax.numpy as jnp
import ml_dtypes
import numpy as np
from jax import lax
from jax.experimental import pallas as pl
from jax.experimental.pallas import tpu as pltpu
from jax.sharding import PartitionSpec as P

NZ = 64
LANES = 128
BLOCKS = 8
WIDTH = 8
TALL = 6
REACH = 6
FOLD = 16
WINDOWS = ((-3, -2, -1, 0, 1, 2, 3), (-2, -1, 1, 2, 3, 4), (-1, 2, 3, 4, 5))


STENCIL = (
    -5369.0 / 1800.0,
    12.0 / 7.0,
    -15.0 / 56.0,
    10.0 / 189.0,
    -1.0 / 112.0,
    2.0 / 1925.0,
    -1.0 / 16632.0,
)


def halves(matrix):
    high = matrix.astype(ml_dtypes.bfloat16)
    low = (matrix - high.astype(np.float64)).astype(ml_dtypes.bfloat16)
    return high, low


def sent_plane(plane_ref):
    row = lax.broadcasted_iota(jnp.int32, (LANES, LANES), 0)
    lane = lax.broadcasted_iota(jnp.int32, (LANES, LANES), 1)
    apart = (row - lane) & (NZ - 1)
    same_half = (row ^ lane) & NZ == 0
    same_block = (row ^ lane) & (NZ - WIDTH) == 0
    parts = [[float(part) for part in halves(np.float64(-0.5 * c))] for c in STENCIL]
    start = 0
    for which in range(2):
        along = jnp.zeros((LANES, LANES), jnp.float32)
        for k in range(1, REACH + 1):
            along = jnp.where((apart == k) | (apart == NZ - k), parts[k][which], along)
        along = jnp.where(same_half, along, 0.0)
        inside = jnp.where(same_block & (row > lane), along, 0.0)
        outside = jnp.where(same_block, 0.0, along)
        columns = slice(which * LANES, (which + 1) * LANES)
        start = 0
        for v, window in enumerate(WINDOWS):
            for other in window:
                tile = []
                for half in range(2):
                    weight = []
                    for out in range(2):
                        there, y = 2 * other + half, 2 * v + out
                        k = abs(there - y)
                        weight.append(parts[k][which] if 1 <= k <= REACH and (there > y or there < 0) else 0.0)
                    above = slice(half * NZ, (half + 1) * NZ)
                    across = jnp.where(lane[above] < NZ, weight[0], weight[1])
                    part = jnp.where(apart[above] == 0, across, 0.0)
                    tile.append(part + inside[above] if other == v else part)
                plane_ref[start : start + LANES, columns] = jnp.concatenate(tile, axis=0).astype(jnp.bfloat16)
                start += LANES
            plane_ref[start : start + LANES, columns] = outside.astype(jnp.bfloat16)
            start += LANES


def placed(x, y, j):
    index = 3 * (x % 3) + y // 2
    half = y % 2 * NZ + j
    return (x // 3, half + index * WIDTH) if index < BLOCKS else (2, half + x // 3 * WIDTH)


def upward_next(layers):
    matrix = np.zeros((2 * LANES, 3 * LANES))
    for x in range(layers):
        for there in range(x + 1):
            for y in range(TALL):
                for j in range(WIDTH):
                    (group, lane), (group_in, lane_in) = placed(x, y, j), placed(there, y, j)
                    if group_in < 2:
                        matrix[group_in * LANES + lane_in, group * LANES + lane] = -0.5 * STENCIL[there + layers - x]
    rest = [np.roll(matrix[:, 2 * LANES :], 2 * WIDTH * i, axis=1) for i in range(4)]
    return tuple(
        turned(np.concatenate(halves(each), axis=1)) for each in (matrix[:, : 2 * LANES], np.concatenate(rest))
    )


def upward_block():
    matrix = np.zeros((2 * LANES, LANES))
    rest = np.zeros((LANES, LANES))
    for x in range(3):
        for y in range(TALL):
            for j in range(WIDTH):
                ends = [(x + k, y, j, k) for k in range(1, 3 - x)]
                ends += [(x, y + k, j, k) for k in range(1, TALL - y)]
                ends += [(x, y, j + k, k) for k in range(1, min(REACH, WIDTH - 1 - j) + 1)]
                group, lane = placed(x, y, j)
                for x_in, y_in, j_in, k in ends:
                    group_in, lane_in = placed(x_in, y_in, j_in)
                    if group == 0:
                        matrix[group_in // 2 * LANES + lane_in, lane] = -0.5 * STENCIL[k]
                    else:
                        for block in range(BLOCKS):
                            rest[lane_in + block * WIDTH, lane + block * WIDTH] = -0.5 * STENCIL[k]
    layers = [np.concatenate([matrix[:LANES], np.roll(matrix[LANES:], 2 * WIDTH * i, axis=0)]) for i in range(4)]
    return tuple(turned(np.concatenate(halves(each), axis=1)) for each in (np.concatenate(layers), rest))


def exchange_blocks(tiles):
    lane = lax.broadcasted_iota(jnp.int16, tiles[0].shape, 1)
    tiles = [pltpu.roll(tile, i * WIDTH, 1) if i else tile for i, tile in enumerate(tiles)]
    for bit in (1, 2, 4):
        upper = (lane & (bit * WIDTH)) != 0
        tiles = [jnp.where(upper, tiles[(i + bit) % BLOCKS], tiles[i]) for i in range(BLOCKS)]
    return [tiles[-c % BLOCKS] for c in range(BLOCKS)]


def turned(matrix):
    rows, columns = matrix.shape
    tiles = matrix.reshape(rows // LANES, LANES, columns // LANES, LANES)
    return jnp.asarray(np.stack([np.roll(tiles, (c * WIDTH, c * WIDTH), (1, 3)).reshape(rows, columns) for c in range(BLOCKS)]))


def coded(potential_ref):
    order = [(x, v) for x in range(6) for v in range(3) if x % 3 + v < 4] + [(2, 2), (5, 2)]
    field = [potential_ref[x : x + 1, v * LANES : (v + 1) * LANES] for x, v in order]
    field = jnp.concatenate(field + [jnp.zeros((3 * BLOCKS - len(field), LANES), jnp.float32)], axis=0)
    pieces = []
    for _ in range(3):
        piece = field.astype(jnp.bfloat16).astype(jnp.float32)
        pieces.append(piece)
        field = field - piece
    high, middle, low = pieces
    mixed = high[16:] + pltpu.roll(middle[16:], 2, 0) + pltpu.roll(low[16:], 4, 0)
    return [high[:16], middle[:16], mixed, low[:8], low[8:16]]


def decoded(codes, block):
    doms, rows, _ = codes.shape
    codes = codes.reshape(doms * rows, LANES)
    block = block[: doms * rows]

    def repeated(at):
        part = jnp.where(block == at, codes, 0.0)
        if at:
            part = pltpu.roll(part, LANES - at * WIDTH, 1)
        for shift in (1, 2, 4):
            part = part + pltpu.roll(part, shift * WIDTH, 1)
        return part.reshape(doms, rows, LANES)

    whole = repeated(3) + repeated(7)
    mixed = repeated(4)[:, 8:]
    mixed = mixed + pltpu.roll(mixed, 6, 1) + pltpu.roll(mixed, 4, 1)
    field = [whole[:, :8] + repeated(5)[:, 8:], whole[:, 8:] + repeated(6)[:, 8:], mixed]
    own = lax.broadcasted_iota(jnp.int32, mixed.shape, 1) == block[: doms * BLOCKS].reshape(mixed.shape)
    return jnp.concatenate([jnp.sum(jnp.where(own, part, 0.0), axis=1, keepdims=True) for part in field], axis=2)


def apply_kernel(layers, bands, rows, group, place_ref, planes_ref, potential_ref, *refs):
    matrices, out_ref, brought, (held, plane, potential, spaced, arrived) = refs[:4], refs[4], refs[5:9], refs[9:]
    size, width = planes_ref.shape
    side, part = rows * LANES, width // 4
    ends = [(width - side, 0, side)] + [(i * part, side + i * part, part) for i in range(4)] + [(0, side + width, side)]
    copies = [
        pltpu.make_async_copy(planes_ref.at[:, pl.ds(start, count)], held.at[:, pl.ds(end, count)], arrived.at[i])
        for i, (start, end, count) in enumerate(ends)
    ]
    copies.append(pltpu.make_async_copy(potential_ref, potential, arrived.at[6]))
    copies += [pltpu.make_async_copy(matrices[i].at[place_ref[2]], brought[i], arrived.at[7 + i]) for i in range(4)]
    for i in (6, 0, 1, 2, 3, 4, 5, 7, 8, 9, 10):
        copies[i].start()
    sent_plane(plane)
    for i in (6, 0, 1):
        copies[i].wait()
    codes = coded(potential)
    lane = lax.broadcasted_iota(jnp.int32, (BLOCKS, LANES), 1)
    steps = width // (group * side)

    @pl.loop(0, steps)
    def _(step):
        for i in range(2, 6):

            @pl.when(step == (i - 1) * steps // 4 - 1)
            def _():
                copies[i].wait()

        base = step * (group * side)
        blank = jnp.zeros((-3 * bands % 16, LANES), jnp.float32)
        lower = (lane[:1] >> 3) & 1 == 0

        def layered(v):
            center = held[:, pl.ds(pl.multiple_of(base + v * LANES, LANES), LANES)].astype(jnp.float32)
            return center[: 3 * bands], center[3 * bands :]

        for v in range((group + 2) * rows):
            low, high = layered(v)
            for which, upper in ((0, low), (1, high)):
                each = jnp.where(lower, high if which == 0 else low, upper)
                spaced[which, :, v * LANES : (v + 1) * LANES] = jnp.concatenate([each, blank], axis=0).astype(jnp.bfloat16)
        applied, start = [], 0
        for v, window in enumerate(WINDOWS):
            stacked = jnp.concatenate(
                [
                    jnp.concatenate(
                        [spaced[at % 2, :, (rows * (at + 1) + i) * LANES : (rows * (at + 1) + i + 1) * LANES] for i in window]
                        + [spaced[1 - at % 2, :, (rows * (at + 1) + v) * LANES : (rows * (at + 1) + v + 1) * LANES]],
                        axis=1,
                    )
                    for at in range(group)
                ],
                axis=0,
            )
            end = start + (len(window) + 1) * LANES
            applied.append(jnp.dot(stacked, plane[start:end], preferred_element_type=jnp.float32))
            start = end
        taller = spaced.shape[1]
        weight = {k: -0.5 * STENCIL[k] for k in range(1, 4)}
        for at in range(group):
            first = lower if at % 2 else ~lower
            across = {i: jnp.where(first, -0.5 * STENCIL[3 + i], -0.5 * STENCIL[3 - i]) for i in range(-2, 3)}
            sent = [[], [], []]
            psi = [[] for _ in range(layers)]
            for v in range(rows):
                place = rows * (at + 1) + v
                low, high = layered(place)
                mine = jnp.where(first, low, high)
                others = jnp.where(first, high, low)
                for x in range(3):
                    slices = [slice(other * bands, (other + 1) * bands) for other in range(3)]
                    total = applied[v][at * taller :][slices[x]]
                    total = total[:, :LANES] + total[:, LANES:]
                    for other in range(3):
                        if other > x:
                            total = total + weight[other - x] * mine[slices[other]]
                        total = total + across[other - x] * others[slices[other]]
                    sent[x].append(total)
                    psi[x].append(low[slices[x]])
                    psi[x + 3].append(high[slices[x]])
            low, high, sent = sum(psi[:3], []), sum(psi[3:], []), sum(sent, [])
            last = [low[8], high[8], sent[8]]
            last = [each[:FOLD] for each in last] + codes[:1] + [
                jnp.concatenate([each[FOLD:], beside], axis=0) for each, beside in zip(last, codes[2:])
            ] + codes[1:2]
            tiles = [jnp.concatenate([low[i], high[i], sent[i], last[i]], axis=0).astype(jnp.bfloat16) for i in range(BLOCKS)]
            for there, tile in enumerate(exchange_blocks(tiles)):
                out_ref[there, step * group + at] = tile

    for copy in copies[7:]:
        copy.wait()


def product_kernel(bands, scaling, place_ref, blocks_ref, *refs):
    next_ref, next_rest_ref, block_ref, rest_ref = refs[:4]
    kept_ref, given_ref, out_ref, psi_ref, half_ref, psi_rest, sent_rest, field, field_rest = refs[4:]
    doms, count = blocks_ref.shape[:2]
    size = count * bands
    even = place_ref[1] == 0
    block = ((lax.broadcasted_iota(jnp.int32, (size, LANES), 1) >> 3) - place_ref[2]) & (BLOCKS - 1)
    quads = doms // 4
    block_short = block.astype(jnp.int16)

    def pair(dom):
        return pl.ds(pl.multiple_of(dom * (2 * LANES), 2 * LANES), 2 * LANES)

    field[...] = 0.5 * decoded(blocks_ref[:, place_ref[0], 3 * bands :, :].astype(jnp.float32), block) - 0.75 * STENCIL[0]

    @pl.loop(0, doms, unroll=8)
    def _(dom):
        quad, i = dom >> 2, dom & 3
        last = blocks_ref[dom, :, 3 * bands :, :].astype(jnp.float32)
        row = field[dom]
        beside = pltpu.roll(last[:, : bands - FOLD], LANES - 4 * WIDTH, 2)
        last = jnp.concatenate([last, beside], axis=1).reshape(size, LANES).astype(jnp.bfloat16)
        mine = block_short & 6 == (2 * i).astype(jnp.int16)
        psi_rest[quad] = jnp.where(mine, pltpu.roll(last, 2 * WIDTH * i, 1), psi_rest[quad])
        sent_rest[quad] = jnp.where(mine, pltpu.roll(last, (2 * WIDTH * (i + 7)) & (LANES - 1), 1), sent_rest[quad])
        field_rest[quad] = jnp.where(block[:1] >> 1 == i, pltpu.roll(row[:, 2 * LANES :], 2 * WIDTH * i, 1), field_rest[quad])
        psi_ref[:, pair(dom)] = jnp.concatenate(
            [blocks_ref[dom, :, at * bands : (at + 1) * bands, :].reshape(size, LANES) for at in range(2)], axis=1
        )

    @pl.loop(0, doms, unroll=8)
    def _(dom):
        i, after = dom & 3, (dom + 1) & (doms - 1)
        psi = psi_ref[:, pair(dom)]
        low, high = psi[:, :LANES], psi[:, LANES:]
        beyond = jnp.dot(psi_ref[:, pair(after)], next_ref[...], preferred_element_type=jnp.float32)
        kept = psi_rest[dom >> 2]
        kept = jnp.where(even, kept, pltpu.roll(kept, LANES - WIDTH, 1))
        kept = jnp.concatenate([jnp.where(even, low, high), kept], axis=1)
        rows = pl.ds(pl.multiple_of(i * (2 * LANES), 2 * LANES), 2 * LANES)
        inner = jnp.dot(kept, block_ref[rows, :], preferred_element_type=jnp.float32)
        inner = inner[:, :LANES] + inner[:, LANES:]
        sent = blocks_ref[dom, :, 2 * bands : 3 * bands, :].reshape(size, LANES).astype(jnp.float32)
        lead = psi_rest[after >> 2]
        from_here = 2 * (after & 3)
        lead = [pltpu.roll(lead, ((place - from_here) * WIDTH) & (LANES - 1), 1).astype(jnp.float32) for place in (2, 5)]
        lead = lead[0] * jnp.where(block[:1] == 2, -0.5 * STENCIL[5], 0.0) + lead[1] * jnp.where(block[:1] == 5, -0.5 * STENCIL[4], 0.0)
        row = field[dom]
        half_low = beyond[:, :LANES] + beyond[:, 2 * LANES : 3 * LANES] + jnp.where(even, inner, sent)
        half_low = half_low + row[:, :LANES] * low.astype(jnp.float32)
        half_high = beyond[:, LANES : 2 * LANES] + beyond[:, 3 * LANES :] + jnp.where(even, sent, inner)
        half_high = half_high + lead + row[:, LANES : 2 * LANES] * high.astype(jnp.float32)
        half_ref[:, pair(dom)] = jnp.concatenate([half_low, half_high], axis=1).astype(jnp.bfloat16)

    for quad in range(quads):
        here, other = psi_rest[quad], psi_rest[(quad + 1) % quads]
        beyond = [psi_ref[:, 2 * ((4 * quad + i + 1) % doms) * LANES :][:, : 2 * LANES] for i in range(4)]
        beyond = jnp.dot(jnp.concatenate(beyond, axis=1), next_rest_ref[...], preferred_element_type=jnp.float32)
        inner = jnp.dot(here, rest_ref[...], preferred_element_type=jnp.float32)
        inner = inner[:, :LANES] + inner[:, LANES:]
        after = jnp.where(block_short >= 6, pltpu.roll(other, 6 * WIDTH, 1), pltpu.roll(here, LANES - 2 * WIDTH, 1))
        half = beyond[:, :LANES] + beyond[:, LANES:] + field_rest[quad] * here.astype(jnp.float32)
        half = half + (-0.5 * STENCIL[6]) * after.astype(jnp.float32)
        half = half + pltpu.roll(after, WIDTH, 1).astype(jnp.float32) * jnp.where(block[:1] & 1 == 1, -0.5 * STENCIL[3], 0.0)
        sent = jnp.where(even, pltpu.roll(sent_rest[quad], WIDTH, 1), sent_rest[quad]).astype(jnp.float32)
        half = half + jnp.where(block & 1 == jnp.where(even, 0, 1), inner, sent)
        place = slice((2 * doms + quad) * LANES, (2 * doms + quad + 1) * LANES)
        psi_ref[:, place] = here
        half_ref[:, place] = half.astype(jnp.bfloat16)

    whole = lax.dot_general(
        psi_ref[...], half_ref[...], (((1,), (1,)), ((), ())), preferred_element_type=jnp.float32
    )
    whole = whole * scaling
    whole = whole + whole.T
    core = place_ref[0] & 1
    for pair in range(count // 2):
        for which in range(2):
            rows = whole[(2 * pair + which) * bands : (2 * pair + which + 1) * bands]
            out_ref[which, pair] = rows
    first, second = out_ref[0], out_ref[1]
    kept_ref[...] = jnp.where(core == 0, first, second)
    given_ref[...] = jnp.where(core == 0, second, first)


def project(bands, scaling, place, received, matrices):
    doms, count, chunk, _ = received.shape
    size = count * bands
    width = (2 * doms + doms // 4) * LANES
    whole = pl.BlockSpec(memory_space=pltpu.VMEM)
    return pl.pallas_call(
        functools.partial(product_kernel, bands, scaling),
        in_specs=[pl.BlockSpec(memory_space=pltpu.SMEM)] + [whole] * 5,
        out_specs=[whole] * 2,
        out_shape=[jax.ShapeDtypeStruct((count // 2, bands, size), jnp.float32)] * 2,
        scratch_shapes=[
            pltpu.VMEM((2, count // 2, bands, size), jnp.float32),
            pltpu.VMEM((size, width), jnp.bfloat16),
            pltpu.VMEM((size, width), jnp.bfloat16),
            pltpu.VMEM((doms // 4, size, LANES), jnp.bfloat16),
            pltpu.VMEM((doms // 4, size, LANES), jnp.bfloat16),
            pltpu.VMEM((doms, 1, 3 * LANES), jnp.float32),
            pltpu.VMEM((doms // 4, 1, LANES), jnp.float32),
        ],
        compiler_params=pltpu.CompilerParams(vmem_limit_bytes=32 * 2**20),
        name="subspace_product",
    )(place, received, *matrices)


def pack(doms, count, place, orbitals, potential):
    bands, layers, cells_row = orbitals.shape
    cells = cells_row // count
    rows = cells // LANES
    chunk = 3 * bands + FOLD
    group = 4
    planes = jnp.transpose(orbitals, (1, 0, 2)).reshape(layers * bands, cells_row)
    matrices = [*upward_next(layers), *upward_block()]
    operands = [pltpu.with_memory_space_constraint(each, pltpu.HBM) for each in (planes, potential, *matrices)]
    return pl.pallas_call(
        functools.partial(apply_kernel, layers, bands, rows, group),
        in_specs=[pl.BlockSpec(memory_space=pltpu.SMEM)] + [pl.BlockSpec(memory_space=pl.ANY)] * 6,
        out_specs=[pl.BlockSpec(memory_space=pltpu.VMEM)] * 5,
        out_shape=[jax.ShapeDtypeStruct((doms, count, chunk, LANES), jnp.bfloat16)]
        + [jax.ShapeDtypeStruct(each.shape[1:], each.dtype) for each in matrices],
        scratch_shapes=[
            pltpu.VMEM((layers * bands, cells_row + 2 * cells), jnp.bfloat16),
            pltpu.VMEM((21 * LANES, 2 * LANES), jnp.bfloat16),
            pltpu.VMEM(potential.shape, jnp.float32),
            pltpu.VMEM((2, 3 * bands + -3 * bands % 16, (group + 2) * cells), jnp.bfloat16),
            pltpu.SemaphoreType.DMA((11,)),
        ],
        compiler_params=pltpu.CompilerParams(vmem_limit_bytes=24 * 2**20),
        name="apply_upward",
    )(place, *operands)


def per_device(orbitals, potential):
    bands, layers, cells_row = orbitals.shape
    count = lax.axis_size("band")
    doms = lax.axis_size("dom")
    size = count * bands
    cells_all = layers * doms * cells_row
    band, dom = lax.axis_index("band"), lax.axis_index("dom")
    place = jnp.stack([band, (band + dom) & 1, dom]).astype(jnp.int32)
    packed, *matrices = pack(doms, count, place, orbitals, potential)
    chunk = packed.shape[2]
    received = lax.all_to_all(packed.reshape(doms * count, chunk, LANES), ("dom", "band"), 0, 0, tiled=True)
    kept, given = project(bands, 1.0 / math.sqrt(cells_all), place, received.reshape(doms, count, chunk, LANES), matrices)
    cores = [(i, i ^ 1) for i in range(count)]
    same_core = [list(range(core, count, 2)) for core in range(2)]
    kept = kept + lax.ppermute(given, "band", cores)
    own_rows = lax.all_to_all(kept, "band", 0, 0, axis_index_groups=same_core, tiled=True).sum(0)
    copies = jnp.broadcast_to(own_rows, (doms, bands, size))
    return lax.all_to_all(copies, "dom", 0, 0, tiled=True).sum(0)


def solution(mesh):
    placed = (P("band", "dom", None), P("dom", "band"))
    return jax.shard_map(
        per_device, mesh=mesh, in_specs=placed, out_specs=P("band", None), check_vma=False
    )
```

```python
import functools
import math

import jax
import jax.numpy as jnp
import ml_dtypes
import numpy as np
from jax import lax
from jax.experimental import pallas as pl
from jax.experimental.pallas import tpu as pltpu
from jax.sharding import PartitionSpec as P

NZ = 64
LANES = 128
BLOCKS = 8
WIDTH = 8
TALL = 6
REACH = 6
FOLD = 16
WINDOWS = ((-3, -2, -1, 0, 1, 2, 3), (-2, -1, 1, 2, 3, 4), (-1, 2, 3, 4, 5))


STENCIL = (
    -5369.0 / 1800.0,
    12.0 / 7.0,
    -15.0 / 56.0,
    10.0 / 189.0,
    -1.0 / 112.0,
    2.0 / 1925.0,
    -1.0 / 16632.0,
)


def halves(matrix):
    high = matrix.astype(ml_dtypes.bfloat16)
    low = (matrix - high.astype(np.float64)).astype(ml_dtypes.bfloat16)
    return high, low


def sent_plane(plane_ref):
    row = lax.broadcasted_iota(jnp.int32, (LANES, LANES), 0)
    lane = lax.broadcasted_iota(jnp.int32, (LANES, LANES), 1)
    apart = (row - lane) & (NZ - 1)
    same_half = (row ^ lane) & NZ == 0
    same_block = (row ^ lane) & (NZ - WIDTH) == 0
    parts = [[float(part) for part in halves(np.float64(-0.5 * c))] for c in STENCIL]
    start = 0
    for which in range(2):
        along = jnp.zeros((LANES, LANES), jnp.float32)
        for k in range(1, REACH + 1):
            along = jnp.where((apart == k) | (apart == NZ - k), parts[k][which], along)
        along = jnp.where(same_half, along, 0.0)
        inside = jnp.where(same_block & (row > lane), along, 0.0)
        outside = jnp.where(same_block, 0.0, along)
        columns = slice(which * LANES, (which + 1) * LANES)
        start = 0
        for v, window in enumerate(WINDOWS):
            for other in window:
                tile = []
                for half in range(2):
                    weight = []
                    for out in range(2):
                        there, y = 2 * other + half, 2 * v + out
                        k = abs(there - y)
                        weight.append(parts[k][which] if 1 <= k <= REACH and (there > y or there < 0) else 0.0)
                    above = slice(half * NZ, (half + 1) * NZ)
                    across = jnp.where(lane[above] < NZ, weight[0], weight[1])
                    part = jnp.where(apart[above] == 0, across, 0.0)
                    tile.append(part + inside[above] if other == v else part)
                plane_ref[start : start + LANES, columns] = jnp.concatenate(tile, axis=0).astype(jnp.bfloat16)
                start += LANES
            plane_ref[start : start + LANES, columns] = outside.astype(jnp.bfloat16)
            start += LANES


def placed(x, y, j):
    index = 3 * (x % 3) + y // 2
    half = y % 2 * NZ + j
    return (x // 3, half + index * WIDTH) if index < BLOCKS else (2, half + x // 3 * WIDTH)


def upward_next(layers):
    matrix = np.zeros((2 * LANES, 3 * LANES))
    for x in range(layers):
        for there in range(x + 1):
            for y in range(TALL):
                for j in range(WIDTH):
                    (group, lane), (group_in, lane_in) = placed(x, y, j), placed(there, y, j)
                    if group_in < 2:
                        matrix[group_in * LANES + lane_in, group * LANES + lane] = -0.5 * STENCIL[there + layers - x]
    rest = [np.roll(matrix[:, 2 * LANES :], 2 * WIDTH * i, axis=1) for i in range(4)]
    return tuple(
        turned(np.concatenate(halves(each), axis=1)) for each in (matrix[:, : 2 * LANES], np.concatenate(rest))
    )


def upward_block():
    matrix = np.zeros((2 * LANES, LANES))
    rest = np.zeros((LANES, LANES))
    for x in range(3):
        for y in range(TALL):
            for j in range(WIDTH):
                ends = [(x + k, y, j, k) for k in range(1, 3 - x)]
                ends += [(x, y + k, j, k) for k in range(1, TALL - y)]
                ends += [(x, y, j + k, k) for k in range(1, min(REACH, WIDTH - 1 - j) + 1)]
                group, lane = placed(x, y, j)
                for x_in, y_in, j_in, k in ends:
                    group_in, lane_in = placed(x_in, y_in, j_in)
                    if group == 0:
                        matrix[group_in // 2 * LANES + lane_in, lane] = -0.5 * STENCIL[k]
                    else:
                        for block in range(BLOCKS):
                            rest[lane_in + block * WIDTH, lane + block * WIDTH] = -0.5 * STENCIL[k]
    layers = [np.concatenate([matrix[:LANES], np.roll(matrix[LANES:], 2 * WIDTH * i, axis=0)]) for i in range(4)]
    return tuple(turned(np.concatenate(halves(each), axis=1)) for each in (np.concatenate(layers), rest))


def exchange_blocks(tiles):
    lane = lax.broadcasted_iota(jnp.int16, tiles[0].shape, 1)
    tiles = [pltpu.roll(tile, i * WIDTH, 1) if i else tile for i, tile in enumerate(tiles)]
    for bit in (1, 2, 4):
        upper = (lane & (bit * WIDTH)) != 0
        tiles = [jnp.where(upper, tiles[(i + bit) % BLOCKS], tiles[i]) for i in range(BLOCKS)]
    return [tiles[-c % BLOCKS] for c in range(BLOCKS)]


def turned(matrix):
    rows, columns = matrix.shape
    tiles = matrix.reshape(rows // LANES, LANES, columns // LANES, LANES)
    return jnp.asarray(np.stack([np.roll(tiles, (c * WIDTH, c * WIDTH), (1, 3)).reshape(rows, columns) for c in range(BLOCKS)]))


def coded(potential_ref):
    order = [(x, v) for x in range(6) for v in range(3) if x % 3 + v < 4] + [(2, 2), (5, 2)]
    field = [potential_ref[x : x + 1, v * LANES : (v + 1) * LANES] for x, v in order]
    field = jnp.concatenate(field + [jnp.zeros((3 * BLOCKS - len(field), LANES), jnp.float32)], axis=0)
    pieces = []
    for _ in range(3):
        piece = field.astype(jnp.bfloat16).astype(jnp.float32)
        pieces.append(piece)
        field = field - piece
    high, middle, low = pieces
    mixed = high[16:] + pltpu.roll(middle[16:], 2, 0) + pltpu.roll(low[16:], 4, 0)
    return [high[:16], middle[:16], mixed, low[:8], low[8:16]]


def decoded(codes, block):
    doms, rows, _ = codes.shape
    codes = codes.reshape(doms * rows, LANES)
    block = block[: doms * rows]

    def repeated(at):
        part = jnp.where(block == at, codes, 0.0)
        if at:
            part = pltpu.roll(part, LANES - at * WIDTH, 1)
        for shift in (1, 2, 4):
            part = part + pltpu.roll(part, shift * WIDTH, 1)
        return part.reshape(doms, rows, LANES)

    whole = repeated(3) + repeated(7)
    mixed = repeated(4)[:, 8:]
    mixed = mixed + pltpu.roll(mixed, 6, 1) + pltpu.roll(mixed, 4, 1)
    field = [whole[:, :8] + repeated(5)[:, 8:], whole[:, 8:] + repeated(6)[:, 8:], mixed]
    own = lax.broadcasted_iota(jnp.int32, mixed.shape, 1) == block[: doms * BLOCKS].reshape(mixed.shape)
    return jnp.concatenate([jnp.sum(jnp.where(own, part, 0.0), axis=1, keepdims=True) for part in field], axis=2)


def apply_kernel(layers, bands, rows, group, place_ref, planes_ref, potential_ref, *refs):
    matrices, out_ref, brought, (held, plane, potential, spaced, arrived) = refs[:4], refs[4], refs[5:9], refs[9:]
    size, width = planes_ref.shape
    side, part = rows * LANES, width // 4
    ends = [(width - side, 0, side)] + [(i * part, side + i * part, part) for i in range(4)] + [(0, side + width, side)]
    copies = [
        pltpu.make_async_copy(planes_ref.at[:, pl.ds(start, count)], held.at[:, pl.ds(end, count)], arrived.at[i])
        for i, (start, end, count) in enumerate(ends)
    ]
    copies.append(pltpu.make_async_copy(potential_ref, potential, arrived.at[6]))
    copies += [pltpu.make_async_copy(matrices[i].at[place_ref[2]], brought[i], arrived.at[7 + i]) for i in range(4)]
    for i in (6, 0, 1, 2, 3, 4, 5, 7, 8, 9, 10):
        copies[i].start()
    sent_plane(plane)
    for i in (6, 0, 1):
        copies[i].wait()
    codes = coded(potential)
    lane = lax.broadcasted_iota(jnp.int32, (BLOCKS, LANES), 1)
    steps = width // (group * side)

    @pl.loop(0, steps)
    def _(step):
        for i in range(2, 6):

            @pl.when(step == (i - 1) * steps // 4 - 1)
            def _():
                copies[i].wait()

        base = step * (group * side)
        blank = jnp.zeros((-3 * bands % 16, LANES), jnp.float32)
        lower = (lane[:1] >> 3) & 1 == 0

        def layered(v):
            center = held[:, pl.ds(pl.multiple_of(base + v * LANES, LANES), LANES)].astype(jnp.float32)
            return center[: 3 * bands], center[3 * bands :]

        for v in range((group + 2) * rows):
            low, high = layered(v)
            for which, upper in ((0, low), (1, high)):
                each = jnp.where(lower, high if which == 0 else low, upper)
                spaced[which, :, v * LANES : (v + 1) * LANES] = jnp.concatenate([each, blank], axis=0).astype(jnp.bfloat16)
        applied, start = [], 0
        for v, window in enumerate(WINDOWS):
            stacked = jnp.concatenate(
                [
                    jnp.concatenate(
                        [spaced[at % 2, :, (rows * (at + 1) + i) * LANES : (rows * (at + 1) + i + 1) * LANES] for i in window]
                        + [spaced[1 - at % 2, :, (rows * (at + 1) + v) * LANES : (rows * (at + 1) + v + 1) * LANES]],
                        axis=1,
                    )
                    for at in range(group)
                ],
                axis=0,
            )
            end = start + (len(window) + 1) * LANES
            applied.append(jnp.dot(stacked, plane[start:end], preferred_element_type=jnp.float32))
            start = end
        taller = spaced.shape[1]
        weight = {k: -0.5 * STENCIL[k] for k in range(1, 4)}
        for at in range(group):
            first = lower if at % 2 else ~lower
            across = {i: jnp.where(first, -0.5 * STENCIL[3 + i], -0.5 * STENCIL[3 - i]) for i in range(-2, 3)}
            sent = [[], [], []]
            psi = [[] for _ in range(layers)]
            for v in range(rows):
                place = rows * (at + 1) + v
                low, high = layered(place)
                mine = jnp.where(first, low, high)
                others = jnp.where(first, high, low)
                for x in range(3):
                    slices = [slice(other * bands, (other + 1) * bands) for other in range(3)]
                    total = applied[v][at * taller :][slices[x]]
                    total = total[:, :LANES] + total[:, LANES:]
                    for other in range(3):
                        if other > x:
                            total = total + weight[other - x] * mine[slices[other]]
                        total = total + across[other - x] * others[slices[other]]
                    sent[x].append(total)
                    psi[x].append(low[slices[x]])
                    psi[x + 3].append(high[slices[x]])
            low, high, sent = sum(psi[:3], []), sum(psi[3:], []), sum(sent, [])
            last = [low[8], high[8], sent[8]]
            last = [each[:FOLD] for each in last] + codes[:1] + [
                jnp.concatenate([each[FOLD:], beside], axis=0) for each, beside in zip(last, codes[2:])
            ] + codes[1:2]
            tiles = [jnp.concatenate([low[i], high[i], sent[i], last[i]], axis=0).astype(jnp.bfloat16) for i in range(BLOCKS)]
            for there, tile in enumerate(exchange_blocks(tiles)):
                out_ref[there, step * group + at] = tile

    for copy in copies[7:]:
        copy.wait()


def product_kernel(bands, scaling, place_ref, blocks_ref, *refs):
    next_ref, next_rest_ref, block_ref, rest_ref = refs[:4]
    kept_ref, given_ref, out_ref, psi_ref, half_ref, psi_rest, sent_rest, field, field_rest = refs[4:]
    doms, count = blocks_ref.shape[:2]
    size = count * bands
    even = place_ref[1] == 0
    block = ((lax.broadcasted_iota(jnp.int32, (size, LANES), 1) >> 3) - place_ref[2]) & (BLOCKS - 1)
    quads = doms // 4
    block_short = block.astype(jnp.int16)

    def pair(dom):
        return slice(dom * 2 * LANES, (dom + 1) * 2 * LANES)

    field[...] = 0.5 * decoded(blocks_ref[:, place_ref[0], 3 * bands :, :].astype(jnp.float32), block) - 0.75 * STENCIL[0]

    for dom in range(doms):
        quad, i = dom >> 2, dom & 3
        last = blocks_ref[dom, :, 3 * bands :, :].astype(jnp.float32)
        row = field[dom]
        beside = pltpu.roll(last[:, : bands - FOLD], LANES - 4 * WIDTH, 2)
        last = jnp.concatenate([last, beside], axis=1).reshape(size, LANES).astype(jnp.bfloat16)
        mine = block_short & 6 == 2 * i
        psi_rest[quad] = jnp.where(mine, pltpu.roll(last, 2 * WIDTH * i, 1), psi_rest[quad])
        sent_rest[quad] = jnp.where(mine, pltpu.roll(last, (2 * WIDTH * (i + 7)) & (LANES - 1), 1), sent_rest[quad])
        field_rest[quad] = jnp.where(block[:1] >> 1 == i, pltpu.roll(row[:, 2 * LANES :], 2 * WIDTH * i, 1), field_rest[quad])
        psi_ref[:, pair(dom)] = jnp.concatenate(
            [blocks_ref[dom, :, at * bands : (at + 1) * bands, :].reshape(size, LANES) for at in range(2)], axis=1
        )

    def apply(dom):
        i, after = dom & 3, (dom + 1) & (doms - 1)
        psi = psi_ref[:, pair(dom)]
        low, high = psi[:, :LANES], psi[:, LANES:]
        beyond = jnp.dot(psi_ref[:, pair(after)], next_ref[...], preferred_element_type=jnp.float32)
        kept = psi_rest[dom >> 2]
        kept = jnp.where(even, kept, pltpu.roll(kept, LANES - WIDTH, 1))
        kept = jnp.concatenate([jnp.where(even, low, high), kept], axis=1)
        rows = slice(i * 2 * LANES, (i + 1) * 2 * LANES)
        inner = jnp.dot(kept, block_ref[rows, :], preferred_element_type=jnp.float32)
        inner = inner[:, :LANES] + inner[:, LANES:]
        sent = blocks_ref[dom, :, 2 * bands : 3 * bands, :].reshape(size, LANES).astype(jnp.float32)
        lead = psi_rest[after >> 2]
        from_here = 2 * (after & 3)
        lead = [pltpu.roll(lead, ((place - from_here) * WIDTH) & (LANES - 1), 1).astype(jnp.float32) for place in (2, 5)]
        lead = lead[0] * jnp.where(block[:1] == 2, -0.5 * STENCIL[5], 0.0) + lead[1] * jnp.where(block[:1] == 5, -0.5 * STENCIL[4], 0.0)
        row = field[dom]
        half_low = beyond[:, :LANES] + beyond[:, 2 * LANES : 3 * LANES] + jnp.where(even, inner, sent)
        half_low = half_low + row[:, :LANES] * low.astype(jnp.float32)
        half_high = beyond[:, LANES : 2 * LANES] + beyond[:, 3 * LANES :] + jnp.where(even, sent, inner)
        half_high = half_high + lead + row[:, LANES : 2 * LANES] * high.astype(jnp.float32)
        half_ref[:, pair(dom)] = jnp.concatenate([half_low, half_high], axis=1).astype(jnp.bfloat16)

    for dom in range(doms // 2):
        apply(dom)
    early = lax.dot_general(
        psi_ref[:, : doms * LANES], half_ref[:, : doms * LANES], (((1,), (1,)), ((), ())), preferred_element_type=jnp.float32
    )
    for dom in range(doms // 2, doms):
        apply(dom)

    for quad in range(quads):
        here, other = psi_rest[quad], psi_rest[(quad + 1) % quads]
        beyond = [psi_ref[:, 2 * ((4 * quad + i + 1) % doms) * LANES :][:, : 2 * LANES] for i in range(4)]
        beyond = jnp.dot(jnp.concatenate(beyond, axis=1), next_rest_ref[...], preferred_element_type=jnp.float32)
        inner = jnp.dot(here, rest_ref[...], preferred_element_type=jnp.float32)
        inner = inner[:, :LANES] + inner[:, LANES:]
        after = jnp.where(block_short >= 6, pltpu.roll(other, 6 * WIDTH, 1), pltpu.roll(here, LANES - 2 * WIDTH, 1))
        half = beyond[:, :LANES] + beyond[:, LANES:] + field_rest[quad] * here.astype(jnp.float32)
        half = half + (-0.5 * STENCIL[6]) * after.astype(jnp.float32)
        half = half + pltpu.roll(after, WIDTH, 1).astype(jnp.float32) * jnp.where(block[:1] & 1 == 1, -0.5 * STENCIL[3], 0.0)
        sent = jnp.where(even, pltpu.roll(sent_rest[quad], WIDTH, 1), sent_rest[quad]).astype(jnp.float32)
        half = half + jnp.where(block & 1 == jnp.where(even, 0, 1), inner, sent)
        place = slice((2 * doms + quad) * LANES, (2 * doms + quad + 1) * LANES)
        psi_ref[:, place] = here
        half_ref[:, place] = half.astype(jnp.bfloat16)

    whole = early
    for start, end in ((doms, 2 * doms + quads),):
        place = slice(start * LANES, end * LANES)
        whole = whole + lax.dot_general(
            psi_ref[:, place], half_ref[:, place], (((1,), (1,)), ((), ())), preferred_element_type=jnp.float32
        )
    whole = whole * scaling
    whole = whole + whole.T
    core = place_ref[0] & 1
    for pair in range(count // 2):
        for which in range(2):
            rows = whole[(2 * pair + which) * bands : (2 * pair + which + 1) * bands]
            out_ref[which, pair] = rows
    first, second = out_ref[0], out_ref[1]
    kept_ref[...] = jnp.where(core == 0, first, second)
    given_ref[...] = jnp.where(core == 0, second, first)


def project(bands, scaling, place, received, matrices):
    doms, count, chunk, _ = received.shape
    size = count * bands
    width = (2 * doms + doms // 4) * LANES
    whole = pl.BlockSpec(memory_space=pltpu.VMEM)
    return pl.pallas_call(
        functools.partial(product_kernel, bands, scaling),
        in_specs=[pl.BlockSpec(memory_space=pltpu.SMEM)] + [whole] * 5,
        out_specs=[whole] * 2,
        out_shape=[jax.ShapeDtypeStruct((count // 2, bands, size), jnp.float32)] * 2,
        scratch_shapes=[
            pltpu.VMEM((2, count // 2, bands, size), jnp.float32),
            pltpu.VMEM((size, width), jnp.bfloat16),
            pltpu.VMEM((size, width), jnp.bfloat16),
            pltpu.VMEM((doms // 4, size, LANES), jnp.bfloat16),
            pltpu.VMEM((doms // 4, size, LANES), jnp.bfloat16),
            pltpu.VMEM((doms, 1, 3 * LANES), jnp.float32),
            pltpu.VMEM((doms // 4, 1, LANES), jnp.float32),
        ],
        compiler_params=pltpu.CompilerParams(vmem_limit_bytes=32 * 2**20),
        name="subspace_product",
    )(place, received, *matrices)


def pack(doms, count, place, orbitals, potential):
    bands, layers, cells_row = orbitals.shape
    cells = cells_row // count
    rows = cells // LANES
    chunk = 3 * bands + FOLD
    group = 4
    planes = jnp.transpose(orbitals, (1, 0, 2)).reshape(layers * bands, cells_row)
    matrices = [*upward_next(layers), *upward_block()]
    operands = [pltpu.with_memory_space_constraint(each, pltpu.HBM) for each in (planes, potential, *matrices)]
    return pl.pallas_call(
        functools.partial(apply_kernel, layers, bands, rows, group),
        in_specs=[pl.BlockSpec(memory_space=pltpu.SMEM)] + [pl.BlockSpec(memory_space=pl.ANY)] * 6,
        out_specs=[pl.BlockSpec(memory_space=pltpu.VMEM)] * 5,
        out_shape=[jax.ShapeDtypeStruct((doms, count, chunk, LANES), jnp.bfloat16)]
        + [jax.ShapeDtypeStruct(each.shape[1:], each.dtype) for each in matrices],
        scratch_shapes=[
            pltpu.VMEM((layers * bands, cells_row + 2 * cells), jnp.bfloat16),
            pltpu.VMEM((21 * LANES, 2 * LANES), jnp.bfloat16),
            pltpu.VMEM(potential.shape, jnp.float32),
            pltpu.VMEM((2, 3 * bands + -3 * bands % 16, (group + 2) * cells), jnp.bfloat16),
            pltpu.SemaphoreType.DMA((11,)),
        ],
        compiler_params=pltpu.CompilerParams(vmem_limit_bytes=24 * 2**20),
        name="apply_upward",
    )(place, *operands)


def per_device(orbitals, potential):
    bands, layers, cells_row = orbitals.shape
    count = lax.axis_size("band")
    doms = lax.axis_size("dom")
    size = count * bands
    cells_all = layers * doms * cells_row
    band, dom = lax.axis_index("band"), lax.axis_index("dom")
    place = jnp.stack([band, (band + dom) & 1, dom]).astype(jnp.int32)
    packed, *matrices = pack(doms, count, place, orbitals, potential)
    chunk = packed.shape[2]
    received = lax.all_to_all(packed.reshape(doms * count, chunk, LANES), ("dom", "band"), 0, 0, tiled=True)
    kept, given = project(bands, 1.0 / math.sqrt(cells_all), place, received.reshape(doms, count, chunk, LANES), matrices)
    cores = [(i, i ^ 1) for i in range(count)]
    same_core = [list(range(core, count, 2)) for core in range(2)]
    kept = kept + lax.ppermute(given, "band", cores)
    own_rows = lax.all_to_all(kept, "band", 0, 0, axis_index_groups=same_core, tiled=True).sum(0)
    copies = jnp.broadcast_to(own_rows, (doms, bands, size))
    return lax.all_to_all(copies, "dom", 0, 0, tiled=True).sum(0)


def solution(mesh):
    placed = (P("band", "dom", None), P("dom", "band"))
    return jax.shard_map(
        per_device, mesh=mesh, in_specs=placed, out_specs=P("band", None), check_vma=False
    )
```

```python
import functools
import math

import jax
import jax.numpy as jnp
import ml_dtypes
import numpy as np
from jax import lax
from jax.experimental import pallas as pl
from jax.experimental.pallas import tpu as pltpu
from jax.sharding import PartitionSpec as P

NZ = 64
LANES = 128
BLOCKS = 8
WIDTH = 8
TALL = 6
REACH = 6
FOLD = 16
WINDOWS = ((-3, -2, -1, 0, 1, 2, 3), (-2, -1, 1, 2, 3, 4), (-1, 2, 3, 4, 5))


STENCIL = (
    -5369.0 / 1800.0,
    12.0 / 7.0,
    -15.0 / 56.0,
    10.0 / 189.0,
    -1.0 / 112.0,
    2.0 / 1925.0,
    -1.0 / 16632.0,
)


def halves(matrix):
    high = matrix.astype(ml_dtypes.bfloat16)
    low = (matrix - high.astype(np.float64)).astype(ml_dtypes.bfloat16)
    return high, low


def sent_plane(plane_ref):
    row = lax.broadcasted_iota(jnp.int32, (LANES, LANES), 0)
    lane = lax.broadcasted_iota(jnp.int32, (LANES, LANES), 1)
    apart = (row - lane) & (NZ - 1)
    same_half = (row ^ lane) & NZ == 0
    same_block = (row ^ lane) & (NZ - WIDTH) == 0
    parts = [[float(part) for part in halves(np.float64(-0.5 * c))] for c in STENCIL]
    start = 0
    for which in range(2):
        along = jnp.zeros((LANES, LANES), jnp.float32)
        for k in range(1, REACH + 1):
            along = jnp.where((apart == k) | (apart == NZ - k), parts[k][which], along)
        along = jnp.where(same_half, along, 0.0)
        inside = jnp.where(same_block & (row > lane), along, 0.0)
        outside = jnp.where(same_block, 0.0, along)
        columns = slice(which * LANES, (which + 1) * LANES)
        start = 0
        for v, window in enumerate(WINDOWS):
            for other in window:
                tile = []
                for half in range(2):
                    weight = []
                    for out in range(2):
                        there, y = 2 * other + half, 2 * v + out
                        k = abs(there - y)
                        weight.append(parts[k][which] if 1 <= k <= REACH and (there > y or there < 0) else 0.0)
                    above = slice(half * NZ, (half + 1) * NZ)
                    across = jnp.where(lane[above] < NZ, weight[0], weight[1])
                    part = jnp.where(apart[above] == 0, across, 0.0)
                    tile.append(part + inside[above] if other == v else part)
                plane_ref[start : start + LANES, columns] = jnp.concatenate(tile, axis=0).astype(jnp.bfloat16)
                start += LANES
            plane_ref[start : start + LANES, columns] = outside.astype(jnp.bfloat16)
            start += LANES


def placed(x, y, j):
    index = 3 * (x % 3) + y // 2
    half = y % 2 * NZ + j
    return (x // 3, half + index * WIDTH) if index < BLOCKS else (2, half + x // 3 * WIDTH)


def upward_next(layers):
    matrix = np.zeros((2 * LANES, 3 * LANES))
    for x in range(layers):
        for there in range(x + 1):
            for y in range(TALL):
                for j in range(WIDTH):
                    (group, lane), (group_in, lane_in) = placed(x, y, j), placed(there, y, j)
                    if group_in < 2:
                        matrix[group_in * LANES + lane_in, group * LANES + lane] = -0.5 * STENCIL[there + layers - x]
    rest = [np.roll(matrix[:, 2 * LANES :], 2 * WIDTH * i, axis=1) for i in range(4)]
    return tuple(
        turned(np.concatenate(halves(each), axis=1)) for each in (matrix[:, : 2 * LANES], np.concatenate(rest))
    )


def upward_block():
    matrix = np.zeros((2 * LANES, LANES))
    rest = np.zeros((LANES, LANES))
    for x in range(3):
        for y in range(TALL):
            for j in range(WIDTH):
                ends = [(x + k, y, j, k) for k in range(1, 3 - x)]
                ends += [(x, y + k, j, k) for k in range(1, TALL - y)]
                ends += [(x, y, j + k, k) for k in range(1, min(REACH, WIDTH - 1 - j) + 1)]
                group, lane = placed(x, y, j)
                for x_in, y_in, j_in, k in ends:
                    group_in, lane_in = placed(x_in, y_in, j_in)
                    if group == 0:
                        matrix[group_in // 2 * LANES + lane_in, lane] = -0.5 * STENCIL[k]
                    else:
                        for block in range(BLOCKS):
                            rest[lane_in + block * WIDTH, lane + block * WIDTH] = -0.5 * STENCIL[k]
    layers = [np.concatenate([matrix[:LANES], np.roll(matrix[LANES:], 2 * WIDTH * i, axis=0)]) for i in range(4)]
    return tuple(turned(np.concatenate(halves(each), axis=1)) for each in (np.concatenate(layers), rest))


def exchange_blocks(tiles):
    lane = lax.broadcasted_iota(jnp.int16, tiles[0].shape, 1)
    tiles = [pltpu.roll(tile, i * WIDTH, 1) if i else tile for i, tile in enumerate(tiles)]
    for bit in (1, 2, 4):
        upper = (lane & (bit * WIDTH)) != 0
        tiles = [jnp.where(upper, tiles[(i + bit) % BLOCKS], tiles[i]) for i in range(BLOCKS)]
    return [tiles[-c % BLOCKS] for c in range(BLOCKS)]


def turned(matrix):
    rows, columns = matrix.shape
    tiles = matrix.reshape(rows // LANES, LANES, columns // LANES, LANES)
    return jnp.asarray(np.stack([np.roll(tiles, (c * WIDTH, c * WIDTH), (1, 3)).reshape(rows, columns) for c in range(BLOCKS)]))


def coded(potential_ref):
    order = [(x, v) for x in range(6) for v in range(3) if x % 3 + v < 4] + [(2, 2), (5, 2)]
    field = [potential_ref[x : x + 1, v * LANES : (v + 1) * LANES] for x, v in order]
    field = jnp.concatenate(field + [jnp.zeros((3 * BLOCKS - len(field), LANES), jnp.float32)], axis=0)
    pieces = []
    for _ in range(3):
        piece = field.astype(jnp.bfloat16).astype(jnp.float32)
        pieces.append(piece)
        field = field - piece
    high, middle, low = pieces
    mixed = high[16:] + pltpu.roll(middle[16:], 2, 0) + pltpu.roll(low[16:], 4, 0)
    return [high[:16], middle[:16], mixed, low[:8], low[8:16]]


def decoded(codes, block):
    doms, rows, _ = codes.shape
    codes = codes.reshape(doms * rows, LANES)
    block = block[: doms * rows]

    def repeated(at):
        part = jnp.where(block == at, codes, 0.0)
        if at:
            part = pltpu.roll(part, LANES - at * WIDTH, 1)
        for shift in (1, 2, 4):
            part = part + pltpu.roll(part, shift * WIDTH, 1)
        return part.reshape(doms, rows, LANES)

    whole = repeated(3) + repeated(7)
    mixed = repeated(4)[:, 8:]
    mixed = mixed + pltpu.roll(mixed, 6, 1) + pltpu.roll(mixed, 4, 1)
    field = [whole[:, :8] + repeated(5)[:, 8:], whole[:, 8:] + repeated(6)[:, 8:], mixed]
    own = lax.broadcasted_iota(jnp.int32, mixed.shape, 1) == block[: doms * BLOCKS].reshape(mixed.shape)
    return jnp.concatenate([jnp.sum(jnp.where(own, part, 0.0), axis=1, keepdims=True) for part in field], axis=2)


def apply_kernel(layers, bands, rows, group, place_ref, planes_ref, potential_ref, *refs):
    matrices, out_ref, brought, (held, plane, potential, spaced, arrived) = refs[:4], refs[4], refs[5:9], refs[9:]
    size, width = planes_ref.shape
    side, part = rows * LANES, width // 4
    ends = [(width - side, 0, side)] + [(i * part, side + i * part, part) for i in range(4)] + [(0, side + width, side)]
    copies = [
        pltpu.make_async_copy(planes_ref.at[:, pl.ds(start, count)], held.at[:, pl.ds(end, count)], arrived.at[i])
        for i, (start, end, count) in enumerate(ends)
    ]
    copies.append(pltpu.make_async_copy(potential_ref, potential, arrived.at[6]))
    copies += [pltpu.make_async_copy(matrices[i].at[place_ref[2]], brought[i], arrived.at[7 + i]) for i in range(4)]
    for i in (6, 0, 1, 2, 3, 4, 5, 7, 8, 9, 10):
        copies[i].start()
    sent_plane(plane)
    for i in (6, 0, 1):
        copies[i].wait()
    codes = coded(potential)
    lane = lax.broadcasted_iota(jnp.int32, (BLOCKS, LANES), 1)
    steps = width // (group * side)

    @pl.loop(0, steps)
    def _(step):
        for i in range(2, 6):

            @pl.when(step == (i - 1) * steps // 4 - 1)
            def _():
                copies[i].wait()

        base = step * (group * side)
        blank = jnp.zeros((-3 * bands % 16, LANES), jnp.float32)
        lower = (lane[:1] >> 3) & 1 == 0

        def layered(v):
            center = held[:, pl.ds(pl.multiple_of(base + v * LANES, LANES), LANES)].astype(jnp.float32)
            return center[: 3 * bands], center[3 * bands :]

        for v in range((group + 2) * rows):
            low, high = layered(v)
            for which, upper in ((0, low), (1, high)):
                each = jnp.where(lower, high if which == 0 else low, upper)
                spaced[which, :, v * LANES : (v + 1) * LANES] = jnp.concatenate([each, blank], axis=0).astype(jnp.bfloat16)
        applied, start = [], 0
        for v, window in enumerate(WINDOWS):
            stacked = jnp.concatenate(
                [
                    jnp.concatenate(
                        [spaced[at % 2, :, (rows * (at + 1) + i) * LANES : (rows * (at + 1) + i + 1) * LANES] for i in window]
                        + [spaced[1 - at % 2, :, (rows * (at + 1) + v) * LANES : (rows * (at + 1) + v + 1) * LANES]],
                        axis=1,
                    )
                    for at in range(group)
                ],
                axis=0,
            )
            end = start + (len(window) + 1) * LANES
            applied.append(jnp.dot(stacked, plane[start:end], preferred_element_type=jnp.float32))
            start = end
        taller = spaced.shape[1]
        weight = {k: -0.5 * STENCIL[k] for k in range(1, 4)}
        for at in range(group):
            first = lower if at % 2 else ~lower
            across = {i: jnp.where(first, -0.5 * STENCIL[3 + i], -0.5 * STENCIL[3 - i]) for i in range(-2, 3)}
            sent = [[], [], []]
            psi = [[] for _ in range(layers)]
            for v in range(rows):
                place = rows * (at + 1) + v
                low, high = layered(place)
                mine = jnp.where(first, low, high)
                others = jnp.where(first, high, low)
                for x in range(3):
                    slices = [slice(other * bands, (other + 1) * bands) for other in range(3)]
                    total = applied[v][at * taller :][slices[x]]
                    total = total[:, :LANES] + total[:, LANES:]
                    for other in range(3):
                        if other > x:
                            total = total + weight[other - x] * mine[slices[other]]
                        total = total + across[other - x] * others[slices[other]]
                    sent[x].append(total)
                    psi[x].append(low[slices[x]])
                    psi[x + 3].append(high[slices[x]])
            low, high, sent = sum(psi[:3], []), sum(psi[3:], []), sum(sent, [])
            last = [low[8], high[8], sent[8]]
            last = [each[:FOLD] for each in last] + codes[:1] + [
                jnp.concatenate([each[FOLD:], beside], axis=0) for each, beside in zip(last, codes[2:])
            ] + codes[1:2]
            tiles = [jnp.concatenate([low[i], high[i], sent[i], last[i]], axis=0).astype(jnp.bfloat16) for i in range(BLOCKS)]
            for there, tile in enumerate(exchange_blocks(tiles)):
                out_ref[there, step * group + at] = tile

    for copy in copies[7:]:
        copy.wait()


def either(first, one, other):
    return one if first else other


def product_of(odd, bands, scaling, place_ref, blocks_ref, *refs):
    next_ref, next_rest_ref, block_ref, rest_ref = refs[:4]
    kept_ref, given_ref, out_ref, psi_ref, half_ref, psi_rest, sent_rest, field, field_rest = refs[4:]
    doms, count = blocks_ref.shape[:2]
    size = count * bands
    even = odd == 0
    block = ((lax.broadcasted_iota(jnp.int32, (size, LANES), 1) >> 3) - place_ref[2]) & (BLOCKS - 1)
    quads = doms // 4
    block_short = block.astype(jnp.int16)

    def pair(dom):
        return slice(dom * 2 * LANES, (dom + 1) * 2 * LANES)

    field[...] = 0.5 * decoded(blocks_ref[:, place_ref[0], 3 * bands :, :].astype(jnp.float32), block) - 0.75 * STENCIL[0]

    for dom in range(doms):
        quad, i = dom >> 2, dom & 3
        last = blocks_ref[dom, :, 3 * bands :, :].astype(jnp.float32)
        row = field[dom]
        beside = pltpu.roll(last[:, : bands - FOLD], LANES - 4 * WIDTH, 2)
        last = jnp.concatenate([last, beside], axis=1).reshape(size, LANES).astype(jnp.bfloat16)
        mine = block_short & 6 == 2 * i
        psi_rest[quad] = jnp.where(mine, pltpu.roll(last, 2 * WIDTH * i, 1), psi_rest[quad])
        sent_rest[quad] = jnp.where(mine, pltpu.roll(last, (2 * WIDTH * (i + 7)) & (LANES - 1), 1), sent_rest[quad])
        field_rest[quad] = jnp.where(block[:1] >> 1 == i, pltpu.roll(row[:, 2 * LANES :], 2 * WIDTH * i, 1), field_rest[quad])
        psi_ref[:, pair(dom)] = jnp.concatenate(
            [blocks_ref[dom, :, at * bands : (at + 1) * bands, :].reshape(size, LANES) for at in range(2)], axis=1
        )

    def apply(dom):
        i, after = dom & 3, (dom + 1) & (doms - 1)
        psi = psi_ref[:, pair(dom)]
        low, high = psi[:, :LANES], psi[:, LANES:]
        beyond = jnp.dot(psi_ref[:, pair(after)], next_ref[...], preferred_element_type=jnp.float32)
        kept = psi_rest[dom >> 2]
        kept = either(even, kept, pltpu.roll(kept, LANES - WIDTH, 1))
        kept = jnp.concatenate([either(even, low, high), kept], axis=1)
        rows = slice(i * 2 * LANES, (i + 1) * 2 * LANES)
        inner = jnp.dot(kept, block_ref[rows, :], preferred_element_type=jnp.float32)
        inner = inner[:, :LANES] + inner[:, LANES:]
        sent = blocks_ref[dom, :, 2 * bands : 3 * bands, :].reshape(size, LANES).astype(jnp.float32)
        lead = psi_rest[after >> 2]
        from_here = 2 * (after & 3)
        lead = [pltpu.roll(lead, ((place - from_here) * WIDTH) & (LANES - 1), 1).astype(jnp.float32) for place in (2, 5)]
        lead = lead[0] * jnp.where(block[:1] == 2, -0.5 * STENCIL[5], 0.0) + lead[1] * jnp.where(block[:1] == 5, -0.5 * STENCIL[4], 0.0)
        row = field[dom]
        half_low = beyond[:, :LANES] + beyond[:, 2 * LANES : 3 * LANES] + either(even, inner, sent)
        half_low = half_low + row[:, :LANES] * low.astype(jnp.float32)
        half_high = beyond[:, LANES : 2 * LANES] + beyond[:, 3 * LANES :] + either(even, sent, inner)
        half_high = half_high + lead + row[:, LANES : 2 * LANES] * high.astype(jnp.float32)
        half_ref[:, pair(dom)] = jnp.concatenate([half_low, half_high], axis=1).astype(jnp.bfloat16)

    for dom in range(doms // 2):
        apply(dom)
    early = lax.dot_general(
        psi_ref[:, : doms * LANES], half_ref[:, : doms * LANES], (((1,), (1,)), ((), ())), preferred_element_type=jnp.float32
    )
    for dom in range(doms // 2, doms):
        apply(dom)

    for quad in range(quads):
        here, other = psi_rest[quad], psi_rest[(quad + 1) % quads]
        beyond = [psi_ref[:, 2 * ((4 * quad + i + 1) % doms) * LANES :][:, : 2 * LANES] for i in range(4)]
        beyond = jnp.dot(jnp.concatenate(beyond, axis=1), next_rest_ref[...], preferred_element_type=jnp.float32)
        inner = jnp.dot(here, rest_ref[...], preferred_element_type=jnp.float32)
        inner = inner[:, :LANES] + inner[:, LANES:]
        after = jnp.where(block_short >= 6, pltpu.roll(other, 6 * WIDTH, 1), pltpu.roll(here, LANES - 2 * WIDTH, 1))
        half = beyond[:, :LANES] + beyond[:, LANES:] + field_rest[quad] * here.astype(jnp.float32)
        half = half + (-0.5 * STENCIL[6]) * after.astype(jnp.float32)
        half = half + pltpu.roll(after, WIDTH, 1).astype(jnp.float32) * jnp.where(block[:1] & 1 == 1, -0.5 * STENCIL[3], 0.0)
        sent = either(even, pltpu.roll(sent_rest[quad], WIDTH, 1), sent_rest[quad]).astype(jnp.float32)
        half = half + jnp.where(block & 1 == either(even, 0, 1), inner, sent)
        place = slice((2 * doms + quad) * LANES, (2 * doms + quad + 1) * LANES)
        psi_ref[:, place] = here
        half_ref[:, place] = half.astype(jnp.bfloat16)

    whole = early
    for start, end in ((doms, 2 * doms + quads),):
        place = slice(start * LANES, end * LANES)
        whole = whole + lax.dot_general(
            psi_ref[:, place], half_ref[:, place], (((1,), (1,)), ((), ())), preferred_element_type=jnp.float32
        )
    whole = whole * scaling
    whole = whole + whole.T
    core = place_ref[0] & 1
    for pair in range(count // 2):
        for which in range(2):
            rows = whole[(2 * pair + which) * bands : (2 * pair + which + 1) * bands]
            out_ref[which, pair] = rows
    first, second = out_ref[0], out_ref[1]
    kept_ref[...] = jnp.where(core == 0, first, second)
    given_ref[...] = jnp.where(core == 0, second, first)


def product_kernel(bands, scaling, place_ref, *refs):
    for odd in range(2):

        @pl.when(place_ref[1] == odd)
        def _():
            product_of(odd, bands, scaling, place_ref, *refs)


def project(bands, scaling, place, received, matrices):
    doms, count, chunk, _ = received.shape
    size = count * bands
    width = (2 * doms + doms // 4) * LANES
    whole = pl.BlockSpec(memory_space=pltpu.VMEM)
    return pl.pallas_call(
        functools.partial(product_kernel, bands, scaling),
        in_specs=[pl.BlockSpec(memory_space=pltpu.SMEM)] + [whole] * 5,
        out_specs=[whole] * 2,
        out_shape=[jax.ShapeDtypeStruct((count // 2, bands, size), jnp.float32)] * 2,
        scratch_shapes=[
            pltpu.VMEM((2, count // 2, bands, size), jnp.float32),
            pltpu.VMEM((size, width), jnp.bfloat16),
            pltpu.VMEM((size, width), jnp.bfloat16),
            pltpu.VMEM((doms // 4, size, LANES), jnp.bfloat16),
            pltpu.VMEM((doms // 4, size, LANES), jnp.bfloat16),
            pltpu.VMEM((doms, 1, 3 * LANES), jnp.float32),
            pltpu.VMEM((doms // 4, 1, LANES), jnp.float32),
        ],
        compiler_params=pltpu.CompilerParams(vmem_limit_bytes=32 * 2**20),
        name="subspace_product",
    )(place, received, *matrices)


def pack(doms, count, place, orbitals, potential):
    bands, layers, cells_row = orbitals.shape
    cells = cells_row // count
    rows = cells // LANES
    chunk = 3 * bands + FOLD
    group = 4
    planes = jnp.transpose(orbitals, (1, 0, 2)).reshape(layers * bands, cells_row)
    matrices = [*upward_next(layers), *upward_block()]
    operands = [pltpu.with_memory_space_constraint(each, pltpu.HBM) for each in (planes, potential, *matrices)]
    return pl.pallas_call(
        functools.partial(apply_kernel, layers, bands, rows, group),
        in_specs=[pl.BlockSpec(memory_space=pltpu.SMEM)] + [pl.BlockSpec(memory_space=pl.ANY)] * 6,
        out_specs=[pl.BlockSpec(memory_space=pltpu.VMEM)] * 5,
        out_shape=[jax.ShapeDtypeStruct((doms, count, chunk, LANES), jnp.bfloat16)]
        + [jax.ShapeDtypeStruct(each.shape[1:], each.dtype) for each in matrices],
        scratch_shapes=[
            pltpu.VMEM((layers * bands, cells_row + 2 * cells), jnp.bfloat16),
            pltpu.VMEM((21 * LANES, 2 * LANES), jnp.bfloat16),
            pltpu.VMEM(potential.shape, jnp.float32),
            pltpu.VMEM((2, 3 * bands + -3 * bands % 16, (group + 2) * cells), jnp.bfloat16),
            pltpu.SemaphoreType.DMA((11,)),
        ],
        compiler_params=pltpu.CompilerParams(vmem_limit_bytes=24 * 2**20),
        name="apply_upward",
    )(place, *operands)


def per_device(orbitals, potential):
    bands, layers, cells_row = orbitals.shape
    count = lax.axis_size("band")
    doms = lax.axis_size("dom")
    size = count * bands
    cells_all = layers * doms * cells_row
    band, dom = lax.axis_index("band"), lax.axis_index("dom")
    place = jnp.stack([band, (band + dom) & 1, dom]).astype(jnp.int32)
    packed, *matrices = pack(doms, count, place, orbitals, potential)
    chunk = packed.shape[2]
    received = lax.all_to_all(packed.reshape(doms * count, chunk, LANES), ("dom", "band"), 0, 0, tiled=True)
    kept, given = project(bands, 1.0 / math.sqrt(cells_all), place, received.reshape(doms, count, chunk, LANES), matrices)
    cores = [(i, i ^ 1) for i in range(count)]
    same_core = [list(range(core, count, 2)) for core in range(2)]
    kept = kept + lax.ppermute(given, "band", cores)
    own_rows = lax.all_to_all(kept, "band", 0, 0, axis_index_groups=same_core, tiled=True).sum(0)
    copies = jnp.broadcast_to(own_rows, (doms, bands, size))
    return lax.all_to_all(copies, "dom", 0, 0, tiled=True).sum(0)


def solution(mesh):
    placed = (P("band", "dom", None), P("dom", "band"))
    return jax.shard_map(
        per_device, mesh=mesh, in_specs=placed, out_specs=P("band", None), check_vma=False
    )
```
